512 devices in a mesh: canal: 64 (over z, y), cross: 8 (over x, core).
Axes of the slice: x: 4, y: 4, z: 16, core: 2. Of those that a mesh axis runs over, the one named last changes fastest.
Arguments:
- conserved: float32 [128, 7, 128, 256], P('canal', None, 'cross'), may hold values from -24 to 24
- iblank: int32 [128, 128, 256], P('canal', 'cross'), may hold values from 0 to 2, as said below
- step_scale: float32 [128, 128, 256], P('canal', 'cross'), may hold values from 0.25 to 8
- speeds: float32 [3, 7], replicated, may hold values from -2 to 2
- left_vectors: float32 [7, 7], replicated, may hold values from -2 to 2
- right_vectors: float32 [7, 7], replicated, may hold values from -2 to 2
Outputs:
- update: float32 [128, 7, 128, 256], P('canal', None, 'cross')
The draws below stay inside these ranges and needn't reach their ends.
Inputs may be any that keep to these rules, and one draw needn't show every extreme that they name: iblank is 0 at hole cells inside the hulls, 2 at fringe cells around them and 1 elsewhere.
All inputs are finite; a program needn't handle non-finite values.
Results may differ from the reference program's by a relative error of at most 0.00012.
Values sent between devices are 32-bit elements; how exact they have to be, the bound alone decides.
A program may use at most 64 MiB of HBM per device.

```python
import math
import jax
import jax.numpy as jnp
from jax import lax

NVAR = 7
NZ = 256
NX = 128
NY = 128


def draw_iblank(key, part):
    key = jax.random.fold_in(key, 11)
    hull_length = max(NX // 4, 1)
    hull_beam = max(NY // 4, 1)
    hull_depth = max(NZ // 4, 1)
    starts_x = jax.random.randint(jax.random.fold_in(key, 1), (2,), 0, NX - hull_length + 1)
    starts_y = jax.random.randint(jax.random.fold_in(key, 2), (2,), 0, NY - hull_beam + 1)
    cells_x = jnp.arange(NX, dtype=jnp.int32)[:, None, None]
    cells_y = jnp.arange(NY, dtype=jnp.int32)[None, :, None]
    cells_z = jnp.arange(NZ, dtype=jnp.int32)[None, None, :]
    holes = jnp.zeros((NX, NY, NZ), dtype=bool)
    nearby = jnp.zeros((NX, NY, NZ), dtype=bool)
    for hull in range(2):
        inside = (cells_x >= starts_x[hull]) & (cells_x < starts_x[hull] + hull_length)
        inside = inside & (cells_y >= starts_y[hull]) & (cells_y < starts_y[hull] + hull_beam)
        inside = inside & (cells_z < hull_depth)
        beside_all = (cells_x >= starts_x[hull] - 2) & (cells_x < starts_x[hull] + hull_length + 2)
        beside_all = beside_all & (cells_y >= starts_y[hull] - 2) & (cells_y < starts_y[hull] + hull_beam + 2)
        beside_all = beside_all & (cells_z < hull_depth + 2)
        holes = holes | inside
        nearby = nearby | beside_all
    fringe = nearby & jnp.logical_not(holes)
    return jnp.where(holes, 0, jnp.where(fringe, 2, 1)).astype(jnp.int32)


def levels(own_key, dims, split, smallest, top_value):
    def one(dim, blocks):
        heights = jax.random.uniform(jax.random.fold_in(jax.random.fold_in(own_key, 6), dim), (blocks,), jnp.float32, smallest / len(split), top_value / len(split))
        return jnp.repeat(jnp.exp(heights), dims[dim] // blocks).reshape((-1,) + (1,) * (len(dims) - dim - 1))

    gain = one(*split[0])
    for cut in split[1:]:
        gain = gain * one(*cut)
    return gain


def normal_values(key, extent, width, limit, split=(), held_as=jnp.bfloat16):
    drawn = jax.random.normal(key, extent, jnp.float32) * width
    if len(split) > 0:
        drawn = levels(key, extent, split, -0.22, 0.18) * drawn
    return jnp.clip(drawn, min=-limit, max=limit).astype(held_as)


def setup_inputs(seed: int = 0) -> dict:
    keys = jax.random.split(jax.random.key(seed), 7)
    conserved = normal_values(keys[0], (NX, NVAR, NY, NZ), 4.0, 24.0, ((0, 64), (2, 8)), jnp.float32)
    iblank = draw_iblank(jax.random.fold_in(keys[6], 71), 0)
    step_scale = jnp.clip(jnp.exp(math.log(8.0) - 3.465736 * jax.random.uniform(keys[2], (NX, NY, NZ), jnp.float32) ** levels(keys[2], (NX, NY, NZ), ((0, 64), (1, 8)), -0.2, 0.2)), 0.25, 8.0)
    speeds = jnp.clip(jax.random.uniform(keys[3], (3, NVAR), jnp.float32, -2.0, 2.0), -2.0, 2.0)
    left_vectors = normal_values(keys[4], (NVAR, NVAR), NVAR ** -0.5, 2.0, (), jnp.float32)
    right_vectors = normal_values(keys[5], (NVAR, NVAR), NVAR ** -0.5, 2.0, (), jnp.float32)
    return {"conserved": conserved, "iblank": iblank, "step_scale": step_scale, "speeds": speeds, "left_vectors": left_vectors, "right_vectors": right_vectors}


EXPLICIT_DAMPING = 1.0 / 32.0
IMPLICIT_DAMPING = 0.25


def eliminate(right_hand, line_scale, forward_speed, backward_speed, carried):
    def advance(running, inputs):
        p_one, q_one, g_one, p_two, q_two, g_two = running
        source, local_scale = inputs
        damping = IMPLICIT_DAMPING * local_scale
        lower_two = -damping
        lower_one = -forward_speed * local_scale - damping
        centre = 1.0 + (forward_speed + backward_speed) * local_scale + 4.0 * damping
        upper_one = -backward_speed * local_scale - damping
        upper_two = -damping
        reduced = lower_one - lower_two * p_two
        pivots = centre - lower_two * q_two - reduced * p_one
        p_new = (upper_one - reduced * q_one) / pivots
        q_new = upper_two / pivots
        g_new = (source - lower_two * g_two - reduced * g_one) / pivots
        return (p_new, q_new, g_new, p_one, q_one, g_one), (p_new, q_new, g_new)
    return lax.scan(advance, carried, (right_hand, line_scale))


def substitute(p_rows, q_rows, g_rows, carried):
    def retreat(running, inputs):
        x_one, x_two = running
        p_row, q_row, g_row = inputs
        solved = g_row - p_row * x_one - q_row * x_two
        return (solved, x_one), solved
    return lax.scan(retreat, carried, (p_rows, q_rows, g_rows), reverse=True)


def solve_lines(right_hand, line_scale, forward_speed, backward_speed):
    nothing = jnp.zeros(right_hand.shape[1:], jnp.float32)
    unused, rows = eliminate(right_hand, line_scale, forward_speed, backward_speed, (nothing, nothing, nothing, nothing, nothing, nothing))
    finished, solution = substitute(rows[0], rows[1], rows[2], (nothing, nothing))
    return solution


def shifted(padded, direction, offset):
    trimmed = padded
    for axis_number in range(3):
        begin = 2 + (offset if axis_number == direction else 0)
        trimmed = lax.slice_in_dim(trimmed, begin, begin + padded.shape[axis_number] - 4, axis=axis_number)
    return trimmed


def flux_of(known_var, speed_row):
    padded = jnp.pad(known_var, 2)
    summed = jnp.zeros(known_var.shape, jnp.float32)
    for direction in range(3):
        plus_one = shifted(padded, direction, 1)
        minus_one = shifted(padded, direction, -1)
        plus_two = shifted(padded, direction, 2)
        minus_two = shifted(padded, direction, -2)
        centred = plus_one - minus_one
        fourth = plus_two - 4.0 * plus_one + 6.0 * known_var - 4.0 * minus_one + minus_two
        summed = summed + (0.5 * speed_row[direction] * centred + EXPLICIT_DAMPING * fourth)
    return summed


def reference(conserved, iblank, step_scale, speeds, left_vectors, right_vectors):
    live_cells = (iblank != 0).astype(jnp.float32)
    field_cells = (iblank == 1).astype(jnp.float32)
    weight_scale = field_cells * step_scale
    known_cells = conserved * live_cells[:, None]

    def one_residual(inputs):
        known_var, speed_row = inputs
        return -(weight_scale * flux_of(known_var, speed_row))

    residual = lax.map(one_residual, (jnp.moveaxis(known_cells, 1, 0), speeds.T))
    characteristic = jnp.einsum("vu,uxyz->vxyz", left_vectors, residual, precision=lax.Precision.HIGHEST)

    def one_solve(inputs):
        values, speed_row = inputs
        for direction in range(3):
            turned = jnp.moveaxis(values, direction, 0)
            turned_scale = jnp.moveaxis(weight_scale, direction, 0)
            solved = solve_lines(turned, turned_scale, jnp.maximum(speed_row[direction], 0.0), jnp.maximum(-speed_row[direction], 0.0))
            values = jnp.moveaxis(solved, 0, direction)
        return values

    third = lax.map(one_solve, (characteristic, speeds.T))
    return jnp.einsum("vu,uxyz->xvyz", right_vectors, third, precision=lax.Precision.HIGHEST)
```

```python
import functools

import jax
import jax.numpy as jnp
from jax import lax
from jax.experimental import pallas as pl
from jax.experimental.pallas import tpu as pltpu
from jax.sharding import PartitionSpec as P

MESH = pl.DeviceIdType.MESH
F32 = jnp.float32
NVAR = 7
TILE = (8, 128)


def partner_of(pair, crosses):
    place = pair // crosses
    rest = lax.rem(pair, crosses)
    if crosses == 8:
        group = 4 * (rest // 4) + lax.rem(lax.rem(rest, 4) + place, 4)
    else:
        group = rest
    return group, place


def pair_of(group, place, crosses):
    if crosses == 8:
        return 8 * place + 4 * (group // 4) + lax.rem(lax.rem(group, 4) - place + 8, 4)
    return crosses * place + group


def factor(w, lower, centre, upper, p_one, q_one, p_two, q_two):
    damping = 0.25 * w
    reduced = w * (0.25 * p_two - lower)
    pivot = (1.0 + centre * w + damping * q_two) - reduced * p_one
    inverse = 1.0 / pivot
    q_new = -damping * inverse
    p_new = -(upper * w + reduced * q_one) * inverse
    return inverse, reduced * inverse, p_new, q_new


def join(swap, g_one, g_two, p_one, q_one, p_two, q_two):
    alpha = 1.0 - q_one * swap(q_two)
    beta = p_one - q_one * swap(p_two)
    gamma = g_one - q_one * swap(g_two)
    alpha_far, beta_far, gamma_far = swap(alpha), swap(beta), swap(gamma)
    return (gamma * alpha_far - beta * gamma_far) / (alpha * alpha_far - beta * beta_far)


def spread(speeds_ref, direction, index):
    forward = jnp.zeros(index.shape, F32)
    backward = jnp.zeros(index.shape, F32)
    for v in range(NVAR):
        speed = speeds_ref[direction, v]
        forward = jnp.where(index == v, jnp.maximum(speed, 0.0), forward)
        backward = jnp.where(index == v, jnp.maximum(-speed, 0.0), backward)
    return forward, backward


def coefficients(speeds_ref, direction, index, top):
    forward, backward = spread(speeds_ref, direction, index)
    lower = jnp.where(top, forward, backward) + 0.25
    upper = jnp.where(top, backward, forward) + 0.25
    return lower, 1.0 + forward + backward, upper


def kernel(
    canals,
    crosses,
    conserved,
    iblank,
    step_scale,
    speeds,
    left,
    right,
    update,
    known,
    weight,
    low_out,
    high_out,
    low_in,
    high_in,
    before,
    after,
    rows,
    send_one,
    recv_one,
    send_two,
    recv_two,
    turned,
    send_three,
    recv_three,
    vertical_weight,
    upright,
    v_inverse,
    v_multiplier,
    v_p,
    v_q,
    work_p,
    work_q,
    work_g,
    v_g,
    halo_send,
    halo_recv,
    send_sems,
    recv_sems,
):
    depth = 4 * canals
    block = min(depth, 128)
    blocks = depth // block
    places = canals // crosses
    half = canals // 2
    c = lax.axis_index("canal")
    k = lax.axis_index("cross")

    barrier = pltpu.get_barrier_semaphore()

    def greet_canal(i, carry):
        pl.semaphore_signal(
            barrier, inc=1, device_id=(lax.rem(c + i, canals), k), device_id_type=MESH
        )
        return carry

    def greet_cross(i, carry):
        pl.semaphore_signal(
            barrier, inc=1, device_id=(c, lax.rem(k + i, crosses)), device_id_type=MESH
        )
        return carry

    lax.fori_loop(1, canals, greet_canal, 0)
    lax.fori_loop(1, crosses, greet_cross, 0)

    for x in range(2):
        flag = iblank[x]
        live = (flag != 0).astype(F32)
        weight[x] = jnp.where(flag == 1, step_scale[x], 0.0)
        for v in range(NVAR):
            cells = conserved[x, v] * live
            known[x, v, 8:24, :] = cells
            low_out[x, v] = cells[0:2]
            high_out[x, v] = cells[14:16]

    pl.semaphore_wait(barrier, canals - 1 + crosses - 1)

    c_next, c_last = lax.rem(c + 1, canals), lax.rem(c + canals - 1, canals)
    k_next, k_last = lax.rem(k + 1, crosses), lax.rem(k + crosses - 1, crosses)
    own = known.at[:, :, pl.ds(8, 16), :]
    halo = []
    for number, (source, target, device) in enumerate(
        (
            (own, before, (c_next, k)),
            (own, after, (c_last, k)),
            (high_out, low_in, (c, k_next)),
            (low_out, high_in, (c, k_last)),
        )
    ):
        copy = pltpu.make_async_remote_copy(
            src_ref=source,
            dst_ref=target,
            send_sem=halo_send.at[number],
            recv_sem=halo_recv.at[number],
            device_id=device,
            device_id_type=MESH,
        )
        copy.start()
        halo.append(copy)

    lane = lax.broadcasted_iota(jnp.int32, TILE, 1)
    sub = lax.broadcasted_iota(jnp.int32, TILE, 0)
    upper_half = sub < 4

    def pack(matrices, target):
        for b in range(blocks):
            first = matrices[0][:, b * block : (b + 1) * block].T
            second = matrices[1][:, b * block : (b + 1) * block].T
            for n in range(block // 8):
                one, two = first[8 * n : 8 * n + 8], second[8 * n : 8 * n + 8]
                chunk = b * (block // 4) + 2 * n
                target[chunk] = jnp.where(upper_half, one, pltpu.roll(two, 4, 0))
                target[chunk + 1] = jnp.where(upper_half, pltpu.roll(one, 4, 0), two)

    pack([jnp.concatenate([weight[x]] * 8, axis=0) for x in range(2)], vertical_weight)
    v_top = lax.rem(sub, 4) == 0
    v_lower, v_centre, v_upper = coefficients(speeds, 2, lane // 16, v_top)

    def v_pick(ref, n, step):
        near, far = ref[n], ref[canals - 1 - n]
        if step:
            near = pltpu.roll(near, 8 - step, 0)
        if step != 2:
            far = pltpu.roll(far, (step + 6) % 8, 0)
        return jnp.where(v_top, near, far)

    def v_factor(n, carry):
        p_one, q_one, p_two, q_two = carry
        for step in range(4):
            w = v_pick(vertical_weight, n, step)
            inverse, multiplier, p_new, q_new = factor(
                w, v_lower, v_centre, v_upper, p_one, q_one, p_two, q_two
            )
            v_inverse[4 * n + step] = inverse
            v_multiplier[4 * n + step] = multiplier
            v_p[4 * n + step] = p_new
            v_q[4 * n + step] = q_new
            p_one, q_one, p_two, q_two = p_new, q_new, p_one, q_one
        return p_one, q_one, p_two, q_two

    zero = jnp.zeros(TILE, F32)
    lax.fori_loop(0, half, v_factor, (zero, zero, zero, zero))

    for copy in halo:
        copy.wait()

    has_last, has_next = c > 0, c < canals - 1
    low_mask, high_mask = k > 0, k < crosses - 1
    zi = lax.broadcasted_iota(jnp.int32, (16, depth), 1)
    for x in range(2):
        fluxes = []
        for v in range(NVAR):
            known[x, v, 6:8, :] = jnp.where(low_mask, low_in[x, v], 0.0)
            known[x, v, 24:26, :] = jnp.where(high_mask, high_in[x, v], 0.0)
            here = known[x, v, 8:24, :]
            if x == 0:
                minus_one = jnp.where(has_last, before[1, v], 0.0)
                minus_two = jnp.where(has_last, before[0, v], 0.0)
                plus_one = known[1, v, 8:24, :]
                plus_two = jnp.where(has_next, after[0, v], 0.0)
            else:
                minus_one = known[0, v, 8:24, :]
                minus_two = jnp.where(has_last, before[1, v], 0.0)
                plus_one = jnp.where(has_next, after[0, v], 0.0)
                plus_two = jnp.where(has_next, after[1, v], 0.0)
            canal_half = 0.5 * speeds[0, v]
            flux = (canal_half - 0.125) * plus_one - (canal_half + 0.125) * minus_one
            outer = plus_two + minus_two
            cross_half = 0.5 * speeds[1, v]
            flux += (cross_half - 0.125) * known[x, v, 9:25, :]
            flux -= (cross_half + 0.125) * known[x, v, 7:23, :]
            outer += known[x, v, 10:26, :] + known[x, v, 6:22, :]
            z_half = 0.5 * speeds[2, v]
            up_one = jnp.where(zi < depth - 1, pltpu.roll(here, depth - 1, 1), 0.0)
            up_two = jnp.where(zi < depth - 2, pltpu.roll(here, depth - 2, 1), 0.0)
            down_one = jnp.where(zi >= 1, pltpu.roll(here, 1, 1), 0.0)
            down_two = jnp.where(zi >= 2, pltpu.roll(here, 2, 1), 0.0)
            flux += (z_half - 0.125) * up_one - (z_half + 0.125) * down_one
            outer += up_two + down_two
            fluxes.append(flux + (outer + 18.0 * here) * (1.0 / 32.0))
        scale = weight[x]
        for v in range(NVAR):
            mixed = left[v, 0] * fluxes[0]
            for u in range(1, NVAR):
                mixed += left[v, u] * fluxes[u]
            rows[x, 16 * v : 16 * v + 16, :] = -(scale * mixed)
        rows[x, 112:128, :] = scale
    pack([rows[0], rows[1]], send_one)

    def send_tile(source, target, device, number):
        pltpu.make_async_remote_copy(
            src_ref=source,
            dst_ref=target,
            send_sem=send_sems.at[number],
            recv_sem=recv_sems.at[number],
            device_id=device,
            device_id_type=MESH,
        ).start()

    def wait_for(ref, count, sem):
        part = ref.at[pl.ds(0, count)]
        pltpu.make_async_copy(part, part, sem).wait()

    def send_canal(i, carry):
        for sign in (1, -1):
            other = lax.rem(c + sign * (half - i) + canals, canals)
            send_tile(send_one.at[other], recv_one.at[c], (other, k), 0)
        return carry

    opposite = lax.rem(c + half, canals)
    send_tile(send_one.at[opposite], recv_one.at[c], (opposite, k), 0)
    lax.fori_loop(1, half, send_canal, 0)
    pltpu.make_async_copy(send_one.at[c], recv_one.at[c], recv_sems.at[0]).start()
    wait_for(recv_one, canals, recv_sems.at[0])

    c_lower, c_centre, c_upper = coefficients(speeds, 0, lane // 16, upper_half)
    is_weight = lane >= 112

    def widen(tile):
        w = jnp.where(is_weight, tile, 0.0)
        w += pltpu.roll(w, 16, 1)
        w += pltpu.roll(w, 32, 1)
        return w + pltpu.roll(w, 64, 1)

    def c_forward(n, carry):
        g_one, p_one, q_one, g_two, p_two, q_two = carry
        near, far = recv_one[n], recv_one[canals - 1 - n]
        outer = jnp.where(upper_half, near, far)
        inner = pltpu.roll(jnp.where(upper_half, far, near), 4, 0)
        for step, source in enumerate((outer, inner)):
            w = widen(source)
            inverse, multiplier, p_new, q_new = factor(
                w, c_lower, c_centre, c_upper, p_one, q_one, p_two, q_two
            )
            g_new = (source * inverse - q_new * g_two) - multiplier * g_one
            work_g[2 * n + step] = g_new
            work_p[2 * n + step] = p_new
            work_q[2 * n + step] = q_new
            g_one, p_one, q_one, g_two, p_two, q_two = g_new, p_new, q_new, g_one, p_one, q_one
        return g_one, p_one, q_one, g_two, p_two, q_two

    g_one, p_one, q_one, g_two, p_two, q_two = lax.fori_loop(0, half, c_forward, (zero,) * 6)

    def c_swap(a):
        return pltpu.roll(a, 4, 0)

    x_one = join(c_swap, g_one, g_two, p_one, q_one, p_two, q_two)
    work_g[canals - 1] = x_one

    def c_back(i, carry):
        x_one, x_two = carry
        n = canals - 2 - i
        solved = (work_g[n] - work_q[n] * x_two) - work_p[n] * x_one
        work_g[n] = solved
        return solved, x_one

    lax.fori_loop(0, canals - 1, c_back, (x_one, c_swap(x_one)))

    def c_restore(n, carry):
        outer, inner = work_g[2 * n], pltpu.roll(work_g[2 * n + 1], 4, 0)
        for pair, tile in (
            (n, jnp.where(upper_half, outer, inner)),
            (canals - 1 - n, jnp.where(upper_half, inner, outer)),
        ):
            group, place = partner_of(pair, crosses)
            send_two[group * places + place] = jnp.where(is_weight, recv_one[pair], tile)
        return carry

    lax.fori_loop(0, half, c_restore, 0)

    def group_of(ref, position):
        return ref.at[pl.ds(position * places, places)]

    def send_cross(i, carry):
        other = lax.rem(k + i, crosses)
        send_tile(group_of(send_two, other), group_of(recv_two, k), (c, other), 1)
        return carry

    lax.fori_loop(1, crosses, send_cross, 0)
    pltpu.make_async_copy(group_of(send_two, k), group_of(recv_two, k), recv_sems.at[1]).start()
    wait_for(recv_two, canals, recv_sems.at[1])

    count = crosses // 2
    lines = 8 * places
    for pair in range(count):
        near = recv_two[pair * places : (pair + 1) * places].reshape(lines, 128)
        other = crosses - 1 - pair
        far = recv_two[other * places : (other + 1) * places].reshape(lines, 128)
        turned[pair] = jnp.concatenate([near, far], axis=0).T

    x_top = lane < lines
    x_lower, x_centre, x_upper = coefficients(speeds, 1, sub, x_top)

    def x_forward(pair, carry):
        g_one, p_one, q_one, g_two, p_two, q_two = carry
        for y in range(16):
            source = jnp.where(
                x_top,
                turned[pair, pl.ds(y, 8, stride=16), :],
                turned[pair, pl.ds(15 - y, 8, stride=16), :],
            )
            w = jnp.broadcast_to(source[7:8], TILE)
            inverse, multiplier, p_new, q_new = factor(
                w, x_lower, x_centre, x_upper, p_one, q_one, p_two, q_two
            )
            g_new = (source * inverse - q_new * g_two) - multiplier * g_one
            work_g[16 * pair + y] = g_new
            work_p[16 * pair + y] = p_new
            work_q[16 * pair + y] = q_new
            g_one, p_one, q_one, g_two, p_two, q_two = g_new, p_new, q_new, g_one, p_one, q_one
        return g_one, p_one, q_one, g_two, p_two, q_two

    g_one, p_one, q_one, g_two, p_two, q_two = lax.fori_loop(0, count, x_forward, (zero,) * 6)

    def x_swap(a):
        return pltpu.roll(a, lines, 1)

    x_one = join(x_swap, g_one, g_two, p_one, q_one, p_two, q_two)
    work_g[16 * count - 1] = x_one

    def x_back(i, carry):
        x_one, x_two = carry
        n = 16 * count - 2 - i
        solved = (work_g[n] - work_q[n] * x_two) - work_p[n] * x_one
        work_g[n] = solved
        return solved, x_one

    lax.fori_loop(0, 16 * count - 1, x_back, (x_one, x_swap(x_one)))

    for pair in range(count):
        for y in range(16):
            turned[pair, pl.ds(y, 8, stride=16), :] = jnp.where(
                x_top, work_g[16 * pair + y], work_g[16 * pair + 15 - y]
            )
        back = turned[pair].T
        send_three[pair * places : (pair + 1) * places] = back[:lines].reshape(places, 8, 128)
        other = crosses - 1 - pair
        send_three[other * places : (other + 1) * places] = back[lines:].reshape(places, 8, 128)

    def send_home(i, carry):
        place, other = i // crosses, lax.rem(i, crosses)
        place = lax.rem(place + c, places)
        other = lax.rem(other + k, crosses)
        target = pair_of(k, place, crosses)
        source = send_three.at[other * places + place]
        itself = jnp.logical_and(target == c, other == k)

        @pl.when(itself)
        def keep():
            pltpu.make_async_copy(source, recv_three.at[c], recv_sems.at[2]).start()

        @pl.when(jnp.logical_not(itself))
        def send():
            send_tile(source, recv_three.at[c], (target, other), 2)

        return carry

    lax.fori_loop(0, canals, send_home, 0)
    wait_for(recv_three, canals, recv_sems.at[2])

    def v_forward(n, carry):
        g_one, g_two = carry
        for step in range(4):
            i = 4 * n + step
            source = v_pick(recv_three, n, step)
            g_new = (source * v_inverse[i] - v_q[i] * g_two) - v_multiplier[i] * g_one
            v_g[i] = g_new
            g_one, g_two = g_new, g_one
        return g_one, g_two

    g_one, g_two = lax.fori_loop(0, half, v_forward, (zero, zero))

    def v_swap(a):
        return jnp.where(v_top, pltpu.roll(a, 7, 0), pltpu.roll(a, 1, 0))

    last = 2 * canals - 1
    x_one = join(v_swap, g_one, g_two, v_p[last], v_q[last], v_p[last - 1], v_q[last - 1])
    v_g[last] = x_one

    def v_back(i, carry):
        x_one, x_two = carry
        n = last - 1 - i
        solved = (v_g[n] - v_q[n] * x_two) - v_p[n] * x_one
        v_g[n] = solved
        return solved, x_one

    lax.fori_loop(0, last, v_back, (x_one, v_swap(x_one)))

    place_of = lax.rem(sub, 4)

    def v_restore(n, carry):
        near, far = [], []
        for part in range(2):
            base = 8 * n + 4 * part
            near_tile = v_g[base]
            far_tile = pltpu.roll(v_g[base], 2, 0)
            for step in range(1, 4):
                near_tile = jnp.where(
                    place_of == step, pltpu.roll(v_g[base + step], step, 0), near_tile
                )
                far_tile = jnp.where(
                    place_of == 3 - step,
                    pltpu.roll(v_g[base + step], (10 - step) % 8, 0),
                    far_tile,
                )
            near.append(near_tile)
            far.append(far_tile)
        far = far[::-1]
        at = pl.multiple_of(8 * n, 8)
        end = pl.multiple_of(depth - 8 - 8 * n, 8)
        for start, (one, two) in ((at, near), (end, far)):
            upright[0, pl.ds(start, 8), :] = jnp.where(upper_half, one, pltpu.roll(two, 4, 0))
            upright[1, pl.ds(start, 8), :] = jnp.where(upper_half, pltpu.roll(one, 4, 0), two)
        return carry

    lax.fori_loop(0, half // 2, v_restore, 0)

    for x in range(2):
        for b in range(blocks):
            third = upright[x, b * block : (b + 1) * block, :].T
            for v in range(NVAR):
                mixed = right[v, 0] * third[0:16]
                for u in range(1, NVAR):
                    mixed += right[v, u] * third[16 * u : 16 * u + 16]
                update[x, v, :, b * block : (b + 1) * block] = mixed

    wait_for(send_one, canals - 1, send_sems.at[0])
    wait_for(send_two, canals - places, send_sems.at[1])
    mine, unused = partner_of(c, crosses)

    @pl.when(mine == k)
    def sent_fewer():
        wait_for(send_three, canals - 1, send_sems.at[2])

    @pl.when(mine != k)
    def sent_all():
        wait_for(send_three, canals, send_sems.at[2])


def solution(mesh):
    canals, crosses = mesh.shape["canal"], mesh.shape["cross"]
    depth = 4 * canals
    cells = (2, NVAR, 16, depth)
    tiles = (canals,) + TILE

    def shards(conserved, iblank, step_scale, speeds, left_vectors, right_vectors):
        vmem = pl.BlockSpec(memory_space=pltpu.VMEM)
        smem = pl.BlockSpec(memory_space=pltpu.SMEM)

        def held(*shape):
            return pltpu.VMEM(shape, F32)

        return pl.pallas_call(
            functools.partial(kernel, canals, crosses),
            out_shape=jax.ShapeDtypeStruct(cells, F32),
            in_specs=[vmem, vmem, vmem, smem, smem, smem],
            out_specs=vmem,
            scratch_shapes=[
                held(2, NVAR, 32, depth),
                held(2, 16, depth),
                held(2, NVAR, 2, depth),
                held(2, NVAR, 2, depth),
                held(2, NVAR, 2, depth),
                held(2, NVAR, 2, depth),
                held(*cells),
                held(*cells),
                held(2, 128, depth),
                held(*tiles),
                held(*tiles),
                held(*tiles),
                held(*tiles),
                held(crosses // 2, 128, 16 * (canals // crosses)),
                held(*tiles),
                held(*tiles),
                held(*tiles),
                held(2, depth, 128),
                held(2 * canals, *TILE),
                held(2 * canals, *TILE),
                held(2 * canals, *TILE),
                held(2 * canals, *TILE),
                held(max(canals, 8 * crosses), *TILE),
                held(max(canals, 8 * crosses), *TILE),
                held(max(canals, 8 * crosses), *TILE),
                held(2 * canals, *TILE),
                pltpu.SemaphoreType.DMA((4,)),
                pltpu.SemaphoreType.DMA((4,)),
                pltpu.SemaphoreType.DMA((3,)),
                pltpu.SemaphoreType.DMA((3,)),
            ],
            compiler_params=pltpu.CompilerParams(
                collective_id=0, has_side_effects=True, vmem_limit_bytes=32 * 1024 * 1024
            ),
        )(conserved, iblank, step_scale, speeds, left_vectors, right_vectors)

    return jax.shard_map(
        shards,
        mesh=mesh,
        in_specs=(
            P("canal", None, "cross", None),
            P("canal", "cross", None),
            P("canal", "cross", None),
            P(),
            P(),
            P(),
        ),
        out_specs=P("canal", None, "cross", None),
        check_vma=False,
    )
```

```python
import functools

import jax
import jax.numpy as jnp
from jax import lax
from jax.experimental import pallas as pl
from jax.experimental.pallas import tpu as pltpu
from jax.sharding import PartitionSpec as P

MESH = pl.DeviceIdType.MESH
F32 = jnp.float32
NVAR = 7
TILE = (8, 128)


def turn_of(canal, crosses):
    return lax.rem(canal // 4, crosses)


def partner_of(pair, canal, crosses):
    return lax.rem(lax.rem(pair, crosses) + turn_of(canal, crosses), crosses), pair // crosses


def pair_of(group, canal, place, crosses):
    return crosses * place + lax.rem(group - turn_of(canal, crosses) + crosses, crosses)


def factor(w, lower, centre, upper, p_one, q_one, p_two, q_two):
    damping = 0.25 * w
    reduced = w * (0.25 * p_two - lower)
    pivot = (1.0 + centre * w + damping * q_two) - reduced * p_one
    inverse = 1.0 / pivot
    q_new = -damping * inverse
    p_new = -(upper * w + reduced * q_one) * inverse
    return inverse, reduced * inverse, p_new, q_new


def join(swap, g_one, g_two, p_one, q_one, p_two, q_two):
    alpha = 1.0 - q_one * swap(q_two)
    beta = p_one - q_one * swap(p_two)
    gamma = g_one - q_one * swap(g_two)
    alpha_far, beta_far, gamma_far = swap(alpha), swap(beta), swap(gamma)
    return (gamma * alpha_far - beta * gamma_far) / (alpha * alpha_far - beta * beta_far)


def spread(speeds_ref, direction, index):
    forward = jnp.zeros(index.shape, F32)
    backward = jnp.zeros(index.shape, F32)
    for v in range(NVAR):
        speed = speeds_ref[direction, v]
        forward = jnp.where(index == v, jnp.maximum(speed, 0.0), forward)
        backward = jnp.where(index == v, jnp.maximum(-speed, 0.0), backward)
    return forward, backward


def coefficients(speeds_ref, direction, index, top):
    forward, backward = spread(speeds_ref, direction, index)
    lower = jnp.where(top, forward, backward) + 0.25
    upper = jnp.where(top, backward, forward) + 0.25
    return lower, 1.0 + forward + backward, upper


def kernel(
    canals,
    crosses,
    conserved_hbm,
    iblank_hbm,
    step_scale_hbm,
    speeds_hbm,
    left_hbm,
    right_hbm,
    update,
    conserved,
    iblank,
    step_scale,
    speeds,
    left,
    right,
    known,
    weight,
    low_out,
    high_out,
    low_in,
    high_in,
    before,
    after,
    rows,
    send_one,
    recv_one,
    send_two,
    recv_two,
    turned,
    send_three,
    recv_three,
    vertical_weight,
    upright,
    v_inverse,
    v_multiplier,
    v_p,
    v_q,
    work_p,
    work_q,
    work_g,
    v_g,
    load_sems,
    halo_send,
    halo_recv,
    send_sems,
    recv_sems,
    entered,
):
    depth = 4 * canals
    block = min(depth, 128)
    blocks = depth // block
    places = canals // crosses
    half = canals // 2
    c = lax.axis_index("canal")
    k = lax.axis_index("cross")

    loads = [
        pltpu.make_async_copy(source, target, load_sems.at[number])
        for number, (source, target) in enumerate(
            (
                (iblank_hbm, iblank),
                (conserved_hbm, conserved),
                (step_scale_hbm, step_scale),
                (speeds_hbm, speeds),
                (left_hbm, left),
                (right_hbm, right),
            )
        )
    ]
    for load in loads:
        load.start()

    barrier = pltpu.get_barrier_semaphore()
    c_next, c_last = lax.rem(c + 1, canals), lax.rem(c + canals - 1, canals)
    k_next, k_last = lax.rem(k + 1, crosses), lax.rem(k + crosses - 1, crosses)

    def greet(device):
        pl.semaphore_signal(barrier, inc=1, device_id=device, device_id_type=MESH)

    def row_mate(i):
        return 4 * (c // 4) + lax.rem(c + i, 4)

    greet((c_next, k))
    greet((c_last, k))
    for i in range(1, canals // 4):
        greet((lax.rem(c + 4 * i, canals), k))
    for i in range(1, crosses):
        greet((c, lax.rem(k + i, crosses)))
    for i in range(1, 4):
        greet((row_mate(i), k))
    for load in loads:
        load.wait()

    for x in range(2):
        flag = iblank[x]
        live = (flag != 0).astype(F32)
        weight[x] = jnp.where(flag == 1, step_scale[x], 0.0)
        for v in range(NVAR):
            cells = conserved[x, v] * live
            known[x, v, 8:24, :] = cells
            low_out[x, v] = cells[0:2]
            high_out[x, v] = cells[14:16]

    pl.semaphore_wait(barrier, 2 + canals // 4 - 1 + crosses - 1 + 3)

    own = known.at[:, :, pl.ds(8, 16), :]
    halo = []
    for number, (source, target, device) in enumerate(
        (
            (own, before, (c_next, k)),
            (own, after, (c_last, k)),
            (high_out, low_in, (c, k_next)),
            (low_out, high_in, (c, k_last)),
        )
    ):
        copy = pltpu.make_async_remote_copy(
            src_ref=source,
            dst_ref=target,
            send_sem=halo_send.at[number],
            recv_sem=halo_recv.at[number],
            device_id=device,
            device_id_type=MESH,
        )
        copy.start()
        halo.append(copy)

    for i in range(1, 4):
        pl.semaphore_signal(entered, inc=1, device_id=(row_mate(i), k), device_id_type=MESH)

    lane = lax.broadcasted_iota(jnp.int32, TILE, 1)
    sub = lax.broadcasted_iota(jnp.int32, TILE, 0)
    upper_half = sub < 4
    zero = jnp.zeros(TILE, F32)

    def pack(matrices, target):
        for b in range(blocks):
            first = matrices[0][:, b * block : (b + 1) * block].T
            second = matrices[1][:, b * block : (b + 1) * block].T
            for n in range(block // 8):
                one, two = first[8 * n : 8 * n + 8], second[8 * n : 8 * n + 8]
                chunk = b * (block // 4) + 2 * n
                target[chunk] = jnp.where(upper_half, one, pltpu.roll(two, 4, 0))
                target[chunk + 1] = jnp.where(upper_half, pltpu.roll(one, 4, 0), two)

    for copy in halo:
        copy.wait()

    has_last, has_next = c > 0, c < canals - 1
    low_mask, high_mask = k > 0, k < crosses - 1
    zi = lax.broadcasted_iota(jnp.int32, (16, depth), 1)
    for x in range(2):
        fluxes = []
        for v in range(NVAR):
            known[x, v, 6:8, :] = jnp.where(low_mask, low_in[x, v], 0.0)
            known[x, v, 24:26, :] = jnp.where(high_mask, high_in[x, v], 0.0)
            here = known[x, v, 8:24, :]
            if x == 0:
                minus_one = jnp.where(has_last, before[1, v], 0.0)
                minus_two = jnp.where(has_last, before[0, v], 0.0)
                plus_one = known[1, v, 8:24, :]
                plus_two = jnp.where(has_next, after[0, v], 0.0)
            else:
                minus_one = known[0, v, 8:24, :]
                minus_two = jnp.where(has_last, before[1, v], 0.0)
                plus_one = jnp.where(has_next, after[0, v], 0.0)
                plus_two = jnp.where(has_next, after[1, v], 0.0)
            canal_half = 0.5 * speeds[0, v]
            flux = (canal_half - 0.125) * plus_one - (canal_half + 0.125) * minus_one
            outer = plus_two + minus_two
            cross_half = 0.5 * speeds[1, v]
            flux += (cross_half - 0.125) * known[x, v, 9:25, :]
            flux -= (cross_half + 0.125) * known[x, v, 7:23, :]
            outer += known[x, v, 10:26, :] + known[x, v, 6:22, :]
            z_half = 0.5 * speeds[2, v]
            up_one = jnp.where(zi < depth - 1, pltpu.roll(here, depth - 1, 1), 0.0)
            up_two = jnp.where(zi < depth - 2, pltpu.roll(here, depth - 2, 1), 0.0)
            down_one = jnp.where(zi >= 1, pltpu.roll(here, 1, 1), 0.0)
            down_two = jnp.where(zi >= 2, pltpu.roll(here, 2, 1), 0.0)
            flux += (z_half - 0.125) * up_one - (z_half + 0.125) * down_one
            outer += up_two + down_two
            fluxes.append(flux + (outer + 18.0 * here) * (1.0 / 32.0))
        scale = weight[x]
        for v in range(NVAR):
            mixed = left[v, 0] * fluxes[0]
            for u in range(1, NVAR):
                mixed += left[v, u] * fluxes[u]
            rows[x, 16 * v : 16 * v + 16, :] = -(scale * mixed)
        rows[x, 112:128, :] = scale
    pack([rows[0], rows[1]], send_one)

    def send_tile(source, target, device, number):
        pltpu.make_async_remote_copy(
            src_ref=source,
            dst_ref=target,
            send_sem=send_sems.at[number],
            recv_sem=recv_sems.at[number],
            device_id=device,
            device_id_type=MESH,
        ).start()

    def wait_for(ref, count, sem):
        part = ref.at[pl.ds(0, count)]
        pltpu.make_async_copy(part, part, sem).wait()

    def retreat(p_rows, q_rows, g_rows, total, span, x_one, x_two, finish):
        def block(base, length, x_one, x_two):
            for i in range(length - 1, -1, -1):
                n = base + i
                solved = (g_rows[n] - q_rows[n] * x_two) - p_rows[n] * x_one
                g_rows[n] = solved
                x_one, x_two = solved, x_one
            return x_one, x_two

        start = total - span
        state = block(start, span - 1, x_one, x_two)
        finish(start)

        def more(i, state):
            base = total - span * (i + 2)
            state = block(base, span, *state)
            finish(base)
            return state

        lax.fori_loop(0, total // span - 1, more, state)

    pl.semaphore_wait(entered, 3)

    def send_canal(i, carry):
        for sign in (1, -1):
            other = lax.rem(c + sign * (half - i) + canals, canals)
            send_tile(send_one.at[other], recv_one.at[c], (other, k), 0)
        return carry

    opposite = lax.rem(c + half, canals)
    send_tile(send_one.at[opposite], recv_one.at[c], (opposite, k), 0)
    lax.fori_loop(1, half, send_canal, 0)
    pltpu.make_async_copy(send_one.at[c], recv_one.at[c], recv_sems.at[0]).start()
    pack([jnp.concatenate([weight[x]] * 8, axis=0) for x in range(2)], vertical_weight)
    v_top = lax.rem(sub, 4) == 0
    v_lower, v_centre, v_upper = coefficients(speeds, 2, lane // 16, v_top)

    def v_pick(ref, n, step):
        near, far = ref[n], ref[canals - 1 - n]
        if step:
            near = pltpu.roll(near, 8 - step, 0)
        if step != 2:
            far = pltpu.roll(far, (step + 6) % 8, 0)
        return jnp.where(v_top, near, far)

    def v_factor(m, carry):
        p_one, q_one, p_two, q_two = carry
        for part in range(8):
            n, step = 2 * m + part // 4, part % 4
            w = v_pick(vertical_weight, n, step)
            inverse, multiplier, p_new, q_new = factor(
                w, v_lower, v_centre, v_upper, p_one, q_one, p_two, q_two
            )
            v_inverse[4 * n + step] = inverse
            v_multiplier[4 * n + step] = multiplier
            v_p[4 * n + step] = p_new
            v_q[4 * n + step] = q_new
            p_one, q_one, p_two, q_two = p_new, q_new, p_one, q_one
        return p_one, q_one, p_two, q_two

    lax.fori_loop(0, half // 2, v_factor, (zero, zero, zero, zero))

    wait_for(recv_one, canals, recv_sems.at[0])

    c_lower, c_centre, c_upper = coefficients(speeds, 0, lane // 16, upper_half)
    is_weight = lane >= 112

    def widen(tile):
        w = jnp.where(is_weight, tile, 0.0)
        w += pltpu.roll(w, 16, 1)
        w += pltpu.roll(w, 32, 1)
        return w + pltpu.roll(w, 64, 1)

    def c_forward(i, carry):
        g_one, p_one, q_one, g_two, p_two, q_two = carry
        for m in range(8):
            n = 8 * i + m
            near, far = recv_one[n], recv_one[canals - 1 - n]
            outer = jnp.where(upper_half, near, far)
            inner = pltpu.roll(jnp.where(upper_half, far, near), 4, 0)
            for step, source in enumerate((outer, inner)):
                w = widen(source)
                inverse, multiplier, p_new, q_new = factor(
                    w, c_lower, c_centre, c_upper, p_one, q_one, p_two, q_two
                )
                g_new = (source * inverse - q_new * g_two) - multiplier * g_one
                work_g[2 * n + step] = g_new
                work_p[2 * n + step] = p_new
                work_q[2 * n + step] = q_new
                g_one, p_one, q_one, g_two, p_two, q_two = g_new, p_new, q_new, g_one, p_one, q_one
        return g_one, p_one, q_one, g_two, p_two, q_two

    g_one, p_one, q_one, g_two, p_two, q_two = lax.fori_loop(0, half // 8, c_forward, (zero,) * 6)

    def c_swap(a):
        return pltpu.roll(a, 4, 0)

    x_one = join(c_swap, g_one, g_two, p_one, q_one, p_two, q_two)
    work_g[canals - 1] = x_one

    def c_restore(start):
        for m in range(8):
            n = start // 2 + m
            outer, inner = work_g[start + 2 * m], pltpu.roll(work_g[start + 2 * m + 1], 4, 0)
            for pair, tile in (
                (n, jnp.where(upper_half, outer, inner)),
                (canals - 1 - n, jnp.where(upper_half, inner, outer)),
            ):
                group, place = partner_of(pair, c, crosses)
                send_two[group * places + place] = jnp.where(is_weight, recv_one[pair], tile)

    retreat(work_p, work_q, work_g, canals, 16, x_one, c_swap(x_one), c_restore)

    def group_of(ref, position):
        return ref.at[pl.ds(position * places, places)]

    def send_cross(i, carry):
        other = lax.rem(k + i, crosses)
        send_tile(group_of(send_two, other), group_of(recv_two, k), (c, other), 1)
        return carry

    lax.fori_loop(1, crosses, send_cross, 0)
    pltpu.make_async_copy(group_of(send_two, k), group_of(recv_two, k), recv_sems.at[1]).start()
    wait_for(recv_two, canals, recv_sems.at[1])

    count = crosses // 2
    lines = 8 * places
    for pair in range(count):
        near = recv_two[pair * places : (pair + 1) * places].reshape(lines, 128)
        other = crosses - 1 - pair
        far = recv_two[other * places : (other + 1) * places].reshape(lines, 128)
        turned[pair] = jnp.concatenate([near, far], axis=0).T

    x_top = lane < lines
    x_lower, x_centre, x_upper = coefficients(speeds, 1, sub, x_top)

    def x_forward(pair, carry):
        g_one, p_one, q_one, g_two, p_two, q_two = carry
        for y in range(16):
            source = jnp.where(
                x_top,
                turned[pair, pl.ds(y, 8, stride=16), :],
                turned[pair, pl.ds(15 - y, 8, stride=16), :],
            )
            w = jnp.broadcast_to(source[7:8], TILE)
            inverse, multiplier, p_new, q_new = factor(
                w, x_lower, x_centre, x_upper, p_one, q_one, p_two, q_two
            )
            g_new = (source * inverse - q_new * g_two) - multiplier * g_one
            work_g[16 * pair + y] = g_new
            work_p[16 * pair + y] = p_new
            work_q[16 * pair + y] = q_new
            g_one, p_one, q_one, g_two, p_two, q_two = g_new, p_new, q_new, g_one, p_one, q_one
        return g_one, p_one, q_one, g_two, p_two, q_two

    g_one, p_one, q_one, g_two, p_two, q_two = lax.fori_loop(0, count, x_forward, (zero,) * 6)

    def x_swap(a):
        return pltpu.roll(a, lines, 1)

    x_one = join(x_swap, g_one, g_two, p_one, q_one, p_two, q_two)
    work_g[16 * count - 1] = x_one

    def send_home(pair):
        def one(i, carry):
            place = lax.rem(i + c, places)
            target = pair_of(k, c, place, crosses)
            for other in (pair, crosses - 1 - pair):
                source = send_three.at[other * places + place]
                itself = jnp.logical_and(target == c, other == k)

                @pl.when(itself)
                def keep():
                    pltpu.make_async_copy(source, recv_three.at[c], recv_sems.at[2]).start()

                @pl.when(jnp.logical_not(itself))
                def send():
                    send_tile(source, recv_three.at[c], (target, other), 2)

            return carry

        lax.fori_loop(0, places, one, 0)

    def x_restore(start):
        pair = start // 16
        for y in range(16):
            turned[pair, pl.ds(y, 8, stride=16), :] = jnp.where(
                x_top, work_g[start + y], work_g[start + 15 - y]
            )
        back = turned[pair].T
        for block in range(places):
            at = 8 * block
            send_three[pair * places + block] = back[at : at + 8]
            send_three[(crosses - 1 - pair) * places + block] = back[lines + at : lines + at + 8]
        send_home(pair)

    retreat(work_p, work_q, work_g, 16 * count, 16, x_one, x_swap(x_one), x_restore)
    wait_for(recv_three, canals, recv_sems.at[2])

    def v_forward(m, carry):
        g_one, g_two = carry
        for step in range(16):
            i = 16 * m + step
            source = v_pick(recv_three, 4 * m + step // 4, step % 4)
            g_new = (source * v_inverse[i] - v_q[i] * g_two) - v_multiplier[i] * g_one
            v_g[i] = g_new
            g_one, g_two = g_new, g_one
        return g_one, g_two

    g_one, g_two = lax.fori_loop(0, half // 4, v_forward, (zero, zero))

    def v_swap(a):
        return jnp.where(v_top, pltpu.roll(a, 7, 0), pltpu.roll(a, 1, 0))

    last = 2 * canals - 1
    x_one = join(v_swap, g_one, g_two, v_p[last], v_q[last], v_p[last - 1], v_q[last - 1])
    v_g[last] = x_one

    place_of = lax.rem(sub, 4)

    def v_chunk(n):
        near, far = [], []
        for part in range(2):
            base = 8 * n + 4 * part
            near_tile = v_g[base]
            far_tile = pltpu.roll(v_g[base], 2, 0)
            for step in range(1, 4):
                near_tile = jnp.where(
                    place_of == step, pltpu.roll(v_g[base + step], step, 0), near_tile
                )
                far_tile = jnp.where(
                    place_of == 3 - step,
                    pltpu.roll(v_g[base + step], (10 - step) % 8, 0),
                    far_tile,
                )
            near.append(near_tile)
            far.append(far_tile)
        far = far[::-1]
        at = pl.multiple_of(8 * n, 8)
        end = pl.multiple_of(depth - 8 - 8 * n, 8)
        for start, (one, two) in ((at, near), (end, far)):
            upright[0, pl.ds(start, 8), :] = jnp.where(upper_half, one, pltpu.roll(two, 4, 0))
            upright[1, pl.ds(start, 8), :] = jnp.where(upper_half, pltpu.roll(one, 4, 0), two)

    def v_restore(start):
        v_chunk(start // 8)
        v_chunk(start // 8 + 1)

    retreat(v_p, v_q, v_g, 2 * canals, 16, x_one, v_swap(x_one), v_restore)

    for x in range(2):
        for b in range(blocks):
            third = upright[x, b * block : (b + 1) * block, :].T
            for v in range(NVAR):
                mixed = right[v, 0] * third[0:16]
                for u in range(1, NVAR):
                    mixed += right[v, u] * third[16 * u : 16 * u + 16]
                update[x, v, :, b * block : (b + 1) * block] = mixed

    wait_for(send_one, canals - 1, send_sems.at[0])
    wait_for(send_two, canals - places, send_sems.at[1])
    mine, unused = partner_of(c, c, crosses)

    @pl.when(mine == k)
    def sent_fewer():
        wait_for(send_three, canals - 1, send_sems.at[2])

    @pl.when(mine != k)
    def sent_all():
        wait_for(send_three, canals, send_sems.at[2])


def solution(mesh):
    canals, crosses = mesh.shape["canal"], mesh.shape["cross"]
    depth = 4 * canals
    cells = (2, NVAR, 16, depth)
    tiles = (canals,) + TILE

    def shards(conserved, iblank, step_scale, speeds, left_vectors, right_vectors):
        vmem = pl.BlockSpec(memory_space=pltpu.VMEM)
        anywhere = pl.BlockSpec(memory_space=pl.ANY)

        def held(*shape):
            return pltpu.VMEM(shape, F32)

        return pl.pallas_call(
            functools.partial(kernel, canals, crosses),
            out_shape=jax.ShapeDtypeStruct(cells, F32),
            in_specs=[anywhere] * 6,
            out_specs=vmem,
            scratch_shapes=[
                held(*cells),
                pltpu.VMEM((2, 16, depth), jnp.int32),
                held(2, 16, depth),
                pltpu.SMEM((3, NVAR), F32),
                pltpu.SMEM((NVAR, NVAR), F32),
                pltpu.SMEM((NVAR, NVAR), F32),
                held(2, NVAR, 32, depth),
                held(2, 16, depth),
                held(2, NVAR, 2, depth),
                held(2, NVAR, 2, depth),
                held(2, NVAR, 2, depth),
                held(2, NVAR, 2, depth),
                held(*cells),
                held(*cells),
                held(2, 128, depth),
                held(*tiles),
                held(*tiles),
                held(*tiles),
                held(*tiles),
                held(crosses // 2, 128, 16 * (canals // crosses)),
                held(*tiles),
                held(*tiles),
                held(*tiles),
                held(2, depth, 128),
                held(2 * canals, *TILE),
                held(2 * canals, *TILE),
                held(2 * canals, *TILE),
                held(2 * canals, *TILE),
                held(max(canals, 8 * crosses), *TILE),
                held(max(canals, 8 * crosses), *TILE),
                held(max(canals, 8 * crosses), *TILE),
                held(2 * canals, *TILE),
                pltpu.SemaphoreType.DMA((6,)),
                pltpu.SemaphoreType.DMA((4,)),
                pltpu.SemaphoreType.DMA((4,)),
                pltpu.SemaphoreType.DMA((3,)),
                pltpu.SemaphoreType.DMA((3,)),
                pltpu.SemaphoreType.REGULAR,
            ],
            compiler_params=pltpu.CompilerParams(
                collective_id=0, has_side_effects=True, vmem_limit_bytes=60 * 1024 * 1024
            ),
        )(conserved, iblank, step_scale, speeds, left_vectors, right_vectors)

    return jax.shard_map(
        shards,
        mesh=mesh,
        in_specs=(
            P("canal", None, "cross", None),
            P("canal", "cross", None),
            P("canal", "cross", None),
            P(),
            P(),
            P(),
        ),
        out_specs=P("canal", None, "cross", None),
        check_vma=False,
    )
```

```python
import functools

import jax
import jax.numpy as jnp
from jax import lax
from jax.experimental import pallas as pl
from jax.experimental.pallas import tpu as pltpu
from jax.sharding import PartitionSpec as P

MESH = pl.DeviceIdType.MESH
F32 = jnp.float32
NVAR = 7
TILE = (8, 128)


def turn_of(canal, crosses):
    return lax.rem(canal // 4, crosses)


def partner_of(pair, canal, crosses):
    return lax.rem(lax.rem(pair, crosses) + turn_of(canal, crosses), crosses), pair // crosses


def pair_of(group, canal, place, crosses):
    return crosses * place + lax.rem(group - turn_of(canal, crosses) + crosses, crosses)


def factor(w, lower, centre, upper, p_one, q_one, p_two, q_two):
    damping = 0.25 * w
    reduced = w * (0.25 * p_two - lower)
    pivot = (1.0 + centre * w + damping * q_two) - reduced * p_one
    inverse = 1.0 / pivot
    q_new = -damping * inverse
    p_new = -(upper * w + reduced * q_one) * inverse
    return inverse, reduced * inverse, p_new, q_new


def join(swap, g_one, g_two, p_one, q_one, p_two, q_two):
    alpha = 1.0 - q_one * swap(q_two)
    beta = p_one - q_one * swap(p_two)
    gamma = g_one - q_one * swap(g_two)
    alpha_far, beta_far, gamma_far = swap(alpha), swap(beta), swap(gamma)
    return (gamma * alpha_far - beta * gamma_far) / (alpha * alpha_far - beta * beta_far)


def spread(speeds_ref, direction, index):
    forward = jnp.zeros(index.shape, F32)
    backward = jnp.zeros(index.shape, F32)
    for v in range(NVAR):
        speed = speeds_ref[direction, v]
        forward = jnp.where(index == v, jnp.maximum(speed, 0.0), forward)
        backward = jnp.where(index == v, jnp.maximum(-speed, 0.0), backward)
    return forward, backward


def coefficients(speeds_ref, direction, index, top):
    forward, backward = spread(speeds_ref, direction, index)
    lower = jnp.where(top, forward, backward) + 0.25
    upper = jnp.where(top, backward, forward) + 0.25
    return lower, 1.0 + forward + backward, upper


def kernel(
    canals,
    crosses,
    conserved_hbm,
    iblank_hbm,
    step_scale_hbm,
    speeds_hbm,
    left_hbm,
    right_hbm,
    update,
    conserved,
    iblank,
    step_scale,
    speeds,
    left,
    right,
    known,
    weight,
    low_out,
    high_out,
    low_in,
    high_in,
    before,
    after,
    partial,
    rows,
    send_one,
    recv_one,
    send_two,
    recv_two,
    turned,
    send_three,
    recv_three,
    vertical_weight,
    upright,
    v_inverse,
    v_multiplier,
    v_p,
    v_q,
    work_p,
    work_q,
    work_g,
    v_g,
    load_sems,
    halo_send,
    halo_recv,
    send_sems,
    recv_sems,
    entered,
):
    depth = 4 * canals
    block = min(depth, 128)
    blocks = depth // block
    places = canals // crosses
    half = canals // 2
    per = canals // blocks
    c = lax.axis_index("canal")
    k = lax.axis_index("cross")

    loads = [
        pltpu.make_async_copy(source, target, load_sems.at[number])
        for number, (source, target) in enumerate(
            (
                (iblank_hbm, iblank),
                (conserved_hbm, conserved),
                (step_scale_hbm, step_scale),
                (speeds_hbm, speeds),
                (left_hbm, left),
                (right_hbm, right),
            )
        )
    ]
    for load in loads:
        load.start()

    barrier = pltpu.get_barrier_semaphore()
    c_next, c_last = lax.rem(c + 1, canals), lax.rem(c + canals - 1, canals)
    k_next, k_last = lax.rem(k + 1, crosses), lax.rem(k + crosses - 1, crosses)

    def greet(device):
        pl.semaphore_signal(barrier, inc=1, device_id=device, device_id_type=MESH)

    def row_mate(i):
        return 4 * (c // 4) + lax.rem(c + i, 4)

    greet((c_next, k))
    greet((c_last, k))
    for i in range(1, canals // 4):
        greet((lax.rem(c + 4 * i, canals), k))
    for i in range(1, crosses):
        greet((c, lax.rem(k + i, crosses)))
    for i in range(1, 4):
        greet((row_mate(i), k))
    for load in loads:
        load.wait()

    for x in range(2):
        flag = iblank[x]
        live = (flag != 0).astype(F32)
        weight[x] = jnp.where(flag == 1, step_scale[x], 0.0)
        for v in range(NVAR):
            cells = conserved[x, v] * live
            known[x, v, 8:24, :] = cells
            low_out[x, v] = cells[0:2]
            high_out[x, v] = cells[14:16]

    pl.semaphore_wait(barrier, 2 + canals // 4 - 1 + crosses - 1 + 3)

    def lanes(ref, b):
        return ref.at[:, :, :, pl.ds(b * block, block)]

    transfers = [(high_out, low_in, (c, k_next)), (low_out, high_in, (c, k_last))]
    for b in range(blocks):
        own = known.at[:, :, pl.ds(8, 16), pl.ds(b * block, block)]
        transfers.append((own, lanes(before, b), (c_next, k)))
        transfers.append((own, lanes(after, b), (c_last, k)))
    halo = []
    for number, (source, target, device) in enumerate(transfers):
        copy = pltpu.make_async_remote_copy(
            src_ref=source,
            dst_ref=target,
            send_sem=halo_send.at[number],
            recv_sem=halo_recv.at[number],
            device_id=device,
            device_id_type=MESH,
        )
        copy.start()
        halo.append(copy)

    for i in range(1, 4):
        pl.semaphore_signal(entered, inc=1, device_id=(row_mate(i), k), device_id_type=MESH)

    lane = lax.broadcasted_iota(jnp.int32, TILE, 1)
    sub = lax.broadcasted_iota(jnp.int32, TILE, 0)
    upper_half = sub < 4
    zero = jnp.zeros(TILE, F32)

    def pack(matrices, target, b):
        first, second = matrices[0].T, matrices[1].T
        for n in range(block // 8):
            one, two = first[8 * n : 8 * n + 8], second[8 * n : 8 * n + 8]
            chunk = b * per + 2 * n
            target[chunk] = jnp.where(upper_half, one, pltpu.roll(two, 4, 0))
            target[chunk + 1] = jnp.where(upper_half, pltpu.roll(one, 4, 0), two)

    halo[0].wait_recv()
    halo[1].wait_recv()
    has_last, has_next = c > 0, c < canals - 1
    low_mask, high_mask = k > 0, k < crosses - 1
    zi = lax.broadcasted_iota(jnp.int32, (16, depth), 1)
    for x in range(2):
        for v in range(NVAR):
            known[x, v, 6:8, :] = jnp.where(low_mask, low_in[x, v], 0.0)
            known[x, v, 24:26, :] = jnp.where(high_mask, high_in[x, v], 0.0)
            here = known[x, v, 8:24, :]
            z_half = 0.5 * speeds[2, v]
            up_one = jnp.where(zi < depth - 1, pltpu.roll(here, depth - 1, 1), 0.0)
            up_two = jnp.where(zi < depth - 2, pltpu.roll(here, depth - 2, 1), 0.0)
            down_one = jnp.where(zi >= 1, pltpu.roll(here, 1, 1), 0.0)
            down_two = jnp.where(zi >= 2, pltpu.roll(here, 2, 1), 0.0)
            flux = (z_half - 0.125) * up_one - (z_half + 0.125) * down_one
            outer = up_two + down_two
            cross_half = 0.5 * speeds[1, v]
            flux += (cross_half - 0.125) * known[x, v, 9:25, :]
            flux -= (cross_half + 0.125) * known[x, v, 7:23, :]
            outer += known[x, v, 10:26, :] + known[x, v, 6:22, :]
            partial[x, v] = flux + (outer + 18.0 * here) * (1.0 / 32.0)

    def send_tile(source, target, device, number):
        pltpu.make_async_remote_copy(
            src_ref=source,
            dst_ref=target,
            send_sem=send_sems.at[number],
            recv_sem=recv_sems.at[number],
            device_id=device,
            device_id_type=MESH,
        ).start()

    def wait_for(ref, count, sem):
        part = ref.at[pl.ds(0, count)]
        pltpu.make_async_copy(part, part, sem).wait()

    def retreat(p_rows, q_rows, g_rows, total, span, x_one, x_two, finish):
        def block(base, length, x_one, x_two):
            for i in range(length - 1, -1, -1):
                n = base + i
                solved = (g_rows[n] - q_rows[n] * x_two) - p_rows[n] * x_one
                g_rows[n] = solved
                x_one, x_two = solved, x_one
            return x_one, x_two

        start = total - span
        state = block(start, span - 1, x_one, x_two)
        finish(start)

        def more(i, state):
            base = total - span * (i + 2)
            state = block(base, span, *state)
            finish(base)
            return state

        lax.fori_loop(0, total // span - 1, more, state)

    pl.semaphore_wait(entered, 3)
    middle = c // blocks

    def to_canal(b, m):
        other = blocks * m + b
        send_tile(send_one.at[b * per + m], recv_one.at[c], (other, k), 0)

    for b in range(blocks):
        halo[2 + 2 * b].wait_recv()
        halo[3 + 2 * b].wait_recv()
        here = slice(b * block, (b + 1) * block)
        for x in range(2):
            fluxes = []
            for v in range(NVAR):
                if x == 0:
                    minus_one = jnp.where(has_last, before[1, v, :, here], 0.0)
                    minus_two = jnp.where(has_last, before[0, v, :, here], 0.0)
                    plus_one = known[1, v, 8:24, here]
                    plus_two = jnp.where(has_next, after[0, v, :, here], 0.0)
                else:
                    minus_one = known[0, v, 8:24, here]
                    minus_two = jnp.where(has_last, before[1, v, :, here], 0.0)
                    plus_one = jnp.where(has_next, after[0, v, :, here], 0.0)
                    plus_two = jnp.where(has_next, after[1, v, :, here], 0.0)
                canal_half = 0.5 * speeds[0, v]
                flux = (canal_half - 0.125) * plus_one - (canal_half + 0.125) * minus_one
                fluxes.append(partial[x, v, :, here] + (flux + (plus_two + minus_two) * (1.0 / 32.0)))
            scale = weight[x, :, here]
            for v in range(NVAR):
                mixed = left[v, 0] * fluxes[0]
                for u in range(1, NVAR):
                    mixed += left[v, u] * fluxes[u]
                rows[x, 16 * v : 16 * v + 16, here] = -(scale * mixed)
            rows[x, 112:128, here] = scale
        pack([rows[x, :, here] for x in range(2)], send_one, b)

        def send_canal(i, carry):
            for sign in (1, -1):
                to_canal(b, lax.rem(middle + sign * (per // 2 - i) + per, per))
            return carry

        to_canal(b, lax.rem(middle + per // 2, per))
        lax.fori_loop(1, per // 2, send_canal, 0)
        mine_now = lax.rem(c, blocks) == b

        @pl.when(mine_now)
        def keep_own():
            pltpu.make_async_copy(
                send_one.at[b * per + middle], recv_one.at[c], recv_sems.at[0]
            ).start()

        @pl.when(jnp.logical_not(mine_now))
        def send_near():
            to_canal(b, middle)

    for b in range(blocks):
        here = slice(b * block, (b + 1) * block)
        pack([jnp.concatenate([weight[x, :, here]] * 8, axis=0) for x in range(2)], vertical_weight, b)
    v_top = lax.rem(sub, 4) == 0
    v_lower, v_centre, v_upper = coefficients(speeds, 2, lane // 16, v_top)

    def v_pick(ref, n, step):
        near, far = ref[n], ref[canals - 1 - n]
        if step:
            near = pltpu.roll(near, 8 - step, 0)
        if step != 2:
            far = pltpu.roll(far, (step + 6) % 8, 0)
        return jnp.where(v_top, near, far)

    def v_factor(m, carry):
        p_one, q_one, p_two, q_two = carry
        for part in range(8):
            n, step = 2 * m + part // 4, part % 4
            w = v_pick(vertical_weight, n, step)
            inverse, multiplier, p_new, q_new = factor(
                w, v_lower, v_centre, v_upper, p_one, q_one, p_two, q_two
            )
            v_inverse[4 * n + step] = inverse
            v_multiplier[4 * n + step] = multiplier
            v_p[4 * n + step] = p_new
            v_q[4 * n + step] = q_new
            p_one, q_one, p_two, q_two = p_new, q_new, p_one, q_one
        return p_one, q_one, p_two, q_two

    lax.fori_loop(0, half // 2, v_factor, (zero, zero, zero, zero))

    wait_for(recv_one, canals, recv_sems.at[0])

    c_lower, c_centre, c_upper = coefficients(speeds, 0, lane // 16, upper_half)
    is_weight = lane >= 112

    def widen(tile):
        w = jnp.where(is_weight, tile, 0.0)
        w += pltpu.roll(w, 16, 1)
        w += pltpu.roll(w, 32, 1)
        return w + pltpu.roll(w, 64, 1)

    def c_forward(i, carry):
        g_one, p_one, q_one, g_two, p_two, q_two = carry
        for m in range(8):
            n = 8 * i + m
            near, far = recv_one[n], recv_one[canals - 1 - n]
            outer = jnp.where(upper_half, near, far)
            inner = pltpu.roll(jnp.where(upper_half, far, near), 4, 0)
            for step, source in enumerate((outer, inner)):
                w = widen(source)
                inverse, multiplier, p_new, q_new = factor(
                    w, c_lower, c_centre, c_upper, p_one, q_one, p_two, q_two
                )
                g_new = (source * inverse - q_new * g_two) - multiplier * g_one
                work_g[2 * n + step] = g_new
                work_p[2 * n + step] = p_new
                work_q[2 * n + step] = q_new
                g_one, p_one, q_one, g_two, p_two, q_two = g_new, p_new, q_new, g_one, p_one, q_one
        return g_one, p_one, q_one, g_two, p_two, q_two

    g_one, p_one, q_one, g_two, p_two, q_two = lax.fori_loop(0, half // 8, c_forward, (zero,) * 6)

    def c_swap(a):
        return pltpu.roll(a, 4, 0)

    x_one = join(c_swap, g_one, g_two, p_one, q_one, p_two, q_two)
    work_g[canals - 1] = x_one

    def c_restore(start):
        for m in range(8):
            n = start // 2 + m
            outer, inner = work_g[start + 2 * m], pltpu.roll(work_g[start + 2 * m + 1], 4, 0)
            for pair, tile in (
                (n, jnp.where(upper_half, outer, inner)),
                (canals - 1 - n, jnp.where(upper_half, inner, outer)),
            ):
                group, place = partner_of(pair, c, crosses)
                send_two[group * places + place] = jnp.where(is_weight, recv_one[pair], tile)

    retreat(work_p, work_q, work_g, canals, 16, x_one, c_swap(x_one), c_restore)

    def group_of(ref, position):
        return ref.at[pl.ds(position * places, places)]

    def send_cross(i, carry):
        other = lax.rem(k + i, crosses)
        send_tile(group_of(send_two, other), group_of(recv_two, k), (c, other), 1)
        return carry

    lax.fori_loop(1, crosses, send_cross, 0)
    pltpu.make_async_copy(group_of(send_two, k), group_of(recv_two, k), recv_sems.at[1]).start()
    wait_for(recv_two, canals, recv_sems.at[1])

    count = crosses // 2
    lines = 8 * places
    for pair in range(count):
        near = recv_two[pair * places : (pair + 1) * places].reshape(lines, 128)
        other = crosses - 1 - pair
        far = recv_two[other * places : (other + 1) * places].reshape(lines, 128)
        turned[pair] = jnp.concatenate([near, far], axis=0).T

    x_top = lane < lines
    x_lower, x_centre, x_upper = coefficients(speeds, 1, sub, x_top)

    def x_forward(pair, carry):
        g_one, p_one, q_one, g_two, p_two, q_two = carry
        for y in range(16):
            source = jnp.where(
                x_top,
                turned[pair, pl.ds(y, 8, stride=16), :],
                turned[pair, pl.ds(15 - y, 8, stride=16), :],
            )
            w = jnp.broadcast_to(source[7:8], TILE)
            inverse, multiplier, p_new, q_new = factor(
                w, x_lower, x_centre, x_upper, p_one, q_one, p_two, q_two
            )
            g_new = (source * inverse - q_new * g_two) - multiplier * g_one
            work_g[16 * pair + y] = g_new
            work_p[16 * pair + y] = p_new
            work_q[16 * pair + y] = q_new
            g_one, p_one, q_one, g_two, p_two, q_two = g_new, p_new, q_new, g_one, p_one, q_one
        return g_one, p_one, q_one, g_two, p_two, q_two

    g_one, p_one, q_one, g_two, p_two, q_two = lax.fori_loop(0, count, x_forward, (zero,) * 6)

    def x_swap(a):
        return pltpu.roll(a, lines, 1)

    x_one = join(x_swap, g_one, g_two, p_one, q_one, p_two, q_two)
    work_g[16 * count - 1] = x_one

    chunk_here = c // blocks + per * lax.rem(c, blocks)

    def send_home(pair):
        def one(i, carry):
            place = lax.rem(i + c, places)
            target = pair_of(k, c, place, crosses)
            for other in (pair, crosses - 1 - pair):
                source = send_three.at[other * places + place]
                itself = jnp.logical_and(target == c, other == k)

                @pl.when(itself)
                def keep():
                    pltpu.make_async_copy(source, recv_three.at[chunk_here], recv_sems.at[2]).start()

                @pl.when(jnp.logical_not(itself))
                def send():
                    send_tile(source, recv_three.at[chunk_here], (target, other), 2)

            return carry

        lax.fori_loop(0, places, one, 0)

    def x_restore(start):
        pair = start // 16
        for y in range(16):
            turned[pair, pl.ds(y, 8, stride=16), :] = jnp.where(
                x_top, work_g[start + y], work_g[start + 15 - y]
            )
        back = turned[pair].T
        for block in range(places):
            at = 8 * block
            send_three[pair * places + block] = back[at : at + 8]
            send_three[(crosses - 1 - pair) * places + block] = back[lines + at : lines + at + 8]
        send_home(pair)

    retreat(work_p, work_q, work_g, 16 * count, 16, x_one, x_swap(x_one), x_restore)
    wait_for(recv_three, canals, recv_sems.at[2])

    def v_forward(m, carry):
        g_one, g_two = carry
        for step in range(16):
            i = 16 * m + step
            source = v_pick(recv_three, 4 * m + step // 4, step % 4)
            g_new = (source * v_inverse[i] - v_q[i] * g_two) - v_multiplier[i] * g_one
            v_g[i] = g_new
            g_one, g_two = g_new, g_one
        return g_one, g_two

    g_one, g_two = lax.fori_loop(0, half // 4, v_forward, (zero, zero))

    def v_swap(a):
        return jnp.where(v_top, pltpu.roll(a, 7, 0), pltpu.roll(a, 1, 0))

    last = 2 * canals - 1
    x_one = join(v_swap, g_one, g_two, v_p[last], v_q[last], v_p[last - 1], v_q[last - 1])
    v_g[last] = x_one

    place_of = lax.rem(sub, 4)

    def v_chunk(n):
        near, far = [], []
        for part in range(2):
            base = 8 * n + 4 * part
            near_tile = v_g[base]
            far_tile = pltpu.roll(v_g[base], 2, 0)
            for step in range(1, 4):
                near_tile = jnp.where(
                    place_of == step, pltpu.roll(v_g[base + step], step, 0), near_tile
                )
                far_tile = jnp.where(
                    place_of == 3 - step,
                    pltpu.roll(v_g[base + step], (10 - step) % 8, 0),
                    far_tile,
                )
            near.append(near_tile)
            far.append(far_tile)
        far = far[::-1]
        at = pl.multiple_of(8 * n, 8)
        end = pl.multiple_of(depth - 8 - 8 * n, 8)
        for start, (one, two) in ((at, near), (end, far)):
            upright[0, pl.ds(start, 8), :] = jnp.where(upper_half, one, pltpu.roll(two, 4, 0))
            upright[1, pl.ds(start, 8), :] = jnp.where(upper_half, pltpu.roll(one, 4, 0), two)

    def v_restore(start):
        v_chunk(start // 8)
        v_chunk(start // 8 + 1)

    retreat(v_p, v_q, v_g, 2 * canals, 16, x_one, v_swap(x_one), v_restore)

    for x in range(2):
        for b in range(blocks):
            third = upright[x, b * block : (b + 1) * block, :].T
            for v in range(NVAR):
                mixed = right[v, 0] * third[0:16]
                for u in range(1, NVAR):
                    mixed += right[v, u] * third[16 * u : 16 * u + 16]
                update[x, v, :, b * block : (b + 1) * block] = mixed

    for copy in halo:
        copy.wait_send()
    wait_for(send_one, canals - 1, send_sems.at[0])
    wait_for(send_two, canals - places, send_sems.at[1])
    mine, unused = partner_of(c, c, crosses)

    @pl.when(mine == k)
    def sent_fewer():
        wait_for(send_three, canals - 1, send_sems.at[2])

    @pl.when(mine != k)
    def sent_all():
        wait_for(send_three, canals, send_sems.at[2])


def solution(mesh):
    canals, crosses = mesh.shape["canal"], mesh.shape["cross"]
    depth = 4 * canals
    cells = (2, NVAR, 16, depth)
    tiles = (canals,) + TILE
    transfers = 2 + 2 * (depth // min(depth, 128))

    def shards(conserved, iblank, step_scale, speeds, left_vectors, right_vectors):
        vmem = pl.BlockSpec(memory_space=pltpu.VMEM)
        anywhere = pl.BlockSpec(memory_space=pl.ANY)

        def held(*shape):
            return pltpu.VMEM(shape, F32)

        return pl.pallas_call(
            functools.partial(kernel, canals, crosses),
            out_shape=jax.ShapeDtypeStruct(cells, F32),
            in_specs=[anywhere] * 6,
            out_specs=vmem,
            scratch_shapes=[
                held(*cells),
                pltpu.VMEM((2, 16, depth), jnp.int32),
                held(2, 16, depth),
                pltpu.SMEM((3, NVAR), F32),
                pltpu.SMEM((NVAR, NVAR), F32),
                pltpu.SMEM((NVAR, NVAR), F32),
                held(2, NVAR, 32, depth),
                held(2, 16, depth),
                held(2, NVAR, 2, depth),
                held(2, NVAR, 2, depth),
                held(2, NVAR, 2, depth),
                held(2, NVAR, 2, depth),
                held(*cells),
                held(*cells),
                held(*cells),
                held(2, 128, depth),
                held(*tiles),
                held(*tiles),
                held(*tiles),
                held(*tiles),
                held(crosses // 2, 128, 16 * (canals // crosses)),
                held(*tiles),
                held(*tiles),
                held(*tiles),
                held(2, depth, 128),
                held(2 * canals, *TILE),
                held(2 * canals, *TILE),
                held(2 * canals, *TILE),
                held(2 * canals, *TILE),
                held(max(canals, 8 * crosses), *TILE),
                held(max(canals, 8 * crosses), *TILE),
                held(max(canals, 8 * crosses), *TILE),
                held(2 * canals, *TILE),
                pltpu.SemaphoreType.DMA((6,)),
                pltpu.SemaphoreType.DMA((transfers,)),
                pltpu.SemaphoreType.DMA((transfers,)),
                pltpu.SemaphoreType.DMA((3,)),
                pltpu.SemaphoreType.DMA((3,)),
                pltpu.SemaphoreType.REGULAR,
            ],
            compiler_params=pltpu.CompilerParams(
                collective_id=0, has_side_effects=True, vmem_limit_bytes=60 * 1024 * 1024
            ),
        )(conserved, iblank, step_scale, speeds, left_vectors, right_vectors)

    return jax.shard_map(
        shards,
        mesh=mesh,
        in_specs=(
            P("canal", None, "cross", None),
            P("canal", "cross", None),
            P("canal", "cross", None),
            P(),
            P(),
            P(),
        ),
        out_specs=P("canal", None, "cross", None),
        check_vma=False,
    )
```

```python
import functools

import jax
import jax.numpy as jnp
from jax import lax
from jax.experimental import pallas as pl
from jax.experimental.pallas import tpu as pltpu
from jax.sharding import PartitionSpec as P

MESH = pl.DeviceIdType.MESH
F32 = jnp.float32
NVAR = 7
TILE = (8, 128)


def turn_of(canal, crosses):
    return lax.rem(canal // 4, crosses)


def partner_of(pair, canal, crosses):
    return lax.rem(lax.rem(pair, crosses) + turn_of(canal, crosses), crosses), pair // crosses


def pair_of(group, canal, place, crosses):
    return crosses * place + lax.rem(group - turn_of(canal, crosses) + crosses, crosses)


def factor(w, lower, centre, upper, p_one, q_one, p_two, q_two):
    damping = 0.25 * w
    reduced = w * (0.25 * p_two - lower)
    pivot = (1.0 + centre * w + damping * q_two) - reduced * p_one
    inverse = pl.reciprocal(pivot, approx=True)
    q_new = -damping * inverse
    p_new = -(upper * w + reduced * q_one) * inverse
    return inverse, reduced * inverse, p_new, q_new


def join(swap, g_one, g_two, p_one, q_one, p_two, q_two):
    alpha = 1.0 - q_one * swap(q_two)
    beta = p_one - q_one * swap(p_two)
    gamma = g_one - q_one * swap(g_two)
    alpha_far, beta_far, gamma_far = swap(alpha), swap(beta), swap(gamma)
    return (gamma * alpha_far - beta * gamma_far) / (alpha * alpha_far - beta * beta_far)


def spread(speeds_ref, direction, index):
    forward = jnp.zeros(index.shape, F32)
    backward = jnp.zeros(index.shape, F32)
    for v in range(NVAR):
        speed = speeds_ref[direction, v]
        forward = jnp.where(index == v, jnp.maximum(speed, 0.0), forward)
        backward = jnp.where(index == v, jnp.maximum(-speed, 0.0), backward)
    return forward, backward


def coefficients(speeds_ref, direction, index, top):
    forward, backward = spread(speeds_ref, direction, index)
    lower = jnp.where(top, forward, backward) + 0.25
    upper = jnp.where(top, backward, forward) + 0.25
    return lower, 1.0 + forward + backward, upper


def kernel(
    canals,
    crosses,
    conserved_hbm,
    iblank_hbm,
    step_scale_hbm,
    speeds_hbm,
    left_hbm,
    right_hbm,
    update,
    conserved,
    iblank,
    step_scale,
    speeds,
    left,
    right,
    known,
    weight,
    low_out,
    high_out,
    low_in,
    high_in,
    before,
    after,
    partial,
    rows,
    send_one,
    recv_one,
    send_two,
    recv_two,
    turned,
    send_three,
    recv_three,
    home,
    vertical_weight,
    upright,
    v_inverse,
    v_multiplier,
    v_p,
    v_q,
    work_p,
    work_q,
    work_g,
    v_g,
    load_sems,
    halo_send,
    halo_recv,
    send_sems,
    recv_sems,
    entered,
):
    depth = 4 * canals
    block = min(depth, 128)
    blocks = depth // block
    places = canals // crosses
    half = canals // 2
    per = canals // blocks
    c = lax.axis_index("canal")
    k = lax.axis_index("cross")

    loads = [
        pltpu.make_async_copy(source, target, load_sems.at[number])
        for number, (source, target) in enumerate(
            (
                (iblank_hbm, iblank),
                (conserved_hbm, conserved),
                (step_scale_hbm, step_scale),
                (speeds_hbm, speeds),
                (left_hbm, left),
                (right_hbm, right),
            )
        )
    ]
    for load in loads:
        load.start()

    barrier = pltpu.get_barrier_semaphore()
    c_next, c_last = lax.rem(c + 1, canals), lax.rem(c + canals - 1, canals)
    k_next, k_last = lax.rem(k + 1, crosses), lax.rem(k + crosses - 1, crosses)

    def greet(device):
        pl.semaphore_signal(barrier, inc=1, device_id=device, device_id_type=MESH)

    def row_mate(i):
        return 4 * (c // 4) + lax.rem(c + i, 4)

    greet((c_next, k))
    greet((c_last, k))
    for i in range(1, canals // 4):
        greet((lax.rem(c + 4 * i, canals), k))
    for i in range(1, crosses):
        greet((c, lax.rem(k + i, crosses)))
    for i in range(1, 4):
        greet((row_mate(i), k))
    for load in loads:
        load.wait()

    for x in range(2):
        flag = iblank[x]
        live = (flag != 0).astype(F32)
        weight[x] = jnp.where(flag == 1, step_scale[x], 0.0)
        for v in range(NVAR):
            cells = conserved[x, v] * live
            known[x, v, 8:24, :] = cells
            low_out[x, v] = cells[0:2]
            high_out[x, v] = cells[14:16]

    pl.semaphore_wait(barrier, 2 + canals // 4 - 1 + crosses - 1 + 3)

    def lanes(ref, b):
        return ref.at[:, :, :, pl.ds(b * block, block)]

    transfers = [(high_out, low_in, (c, k_next)), (low_out, high_in, (c, k_last))]
    for b in range(blocks):
        own = known.at[:, :, pl.ds(8, 16), pl.ds(b * block, block)]
        transfers.append((own, lanes(before, b), (c_next, k)))
        transfers.append((own, lanes(after, b), (c_last, k)))
    halo = []
    for number, (source, target, device) in enumerate(transfers):
        copy = pltpu.make_async_remote_copy(
            src_ref=source,
            dst_ref=target,
            send_sem=halo_send.at[number],
            recv_sem=halo_recv.at[number],
            device_id=device,
            device_id_type=MESH,
        )
        copy.start()
        halo.append(copy)

    for i in range(1, 4):
        pl.semaphore_signal(entered, inc=1, device_id=(row_mate(i), k), device_id_type=MESH)

    lane = lax.broadcasted_iota(jnp.int32, TILE, 1)
    sub = lax.broadcasted_iota(jnp.int32, TILE, 0)
    upper_half = sub < 4
    zero = jnp.zeros(TILE, F32)

    def pack(matrices, target, b):
        first, second = matrices[0].T, matrices[1].T
        for n in range(block // 8):
            one, two = first[8 * n : 8 * n + 8], second[8 * n : 8 * n + 8]
            chunk = b * per + 2 * n
            target[chunk] = jnp.where(upper_half, one, pltpu.roll(two, 4, 0))
            target[chunk + 1] = jnp.where(upper_half, pltpu.roll(one, 4, 0), two)

    halo[0].wait_recv()
    halo[1].wait_recv()
    has_last, has_next = c > 0, c < canals - 1
    low_mask, high_mask = k > 0, k < crosses - 1
    zi = lax.broadcasted_iota(jnp.int32, (16, depth), 1)
    for x in range(2):
        for v in range(NVAR):
            known[x, v, 6:8, :] = jnp.where(low_mask, low_in[x, v], 0.0)
            known[x, v, 24:26, :] = jnp.where(high_mask, high_in[x, v], 0.0)
            here = known[x, v, 8:24, :]
            z_half = 0.5 * speeds[2, v]
            up_one = jnp.where(zi < depth - 1, pltpu.roll(here, depth - 1, 1), 0.0)
            up_two = jnp.where(zi < depth - 2, pltpu.roll(here, depth - 2, 1), 0.0)
            down_one = jnp.where(zi >= 1, pltpu.roll(here, 1, 1), 0.0)
            down_two = jnp.where(zi >= 2, pltpu.roll(here, 2, 1), 0.0)
            flux = (z_half - 0.125) * up_one - (z_half + 0.125) * down_one
            outer = up_two + down_two
            cross_half = 0.5 * speeds[1, v]
            flux += (cross_half - 0.125) * known[x, v, 9:25, :]
            flux -= (cross_half + 0.125) * known[x, v, 7:23, :]
            outer += known[x, v, 10:26, :] + known[x, v, 6:22, :]
            partial[x, v] = flux + (outer + 18.0 * here) * (1.0 / 32.0)

    def send_tile(source, target, device, number):
        pltpu.make_async_remote_copy(
            src_ref=source,
            dst_ref=target,
            send_sem=send_sems.at[number],
            recv_sem=recv_sems.at[number],
            device_id=device,
            device_id_type=MESH,
        ).start()

    def wait_for(ref, count, sem):
        part = ref.at[pl.ds(0, count)]
        pltpu.make_async_copy(part, part, sem).wait()

    def retreat(p_rows, q_rows, g_rows, total, span, x_one, x_two, finish):
        def block(base, length, x_one, x_two):
            for i in range(length - 1, -1, -1):
                n = base + i
                solved = (g_rows[n] - q_rows[n] * x_two) - p_rows[n] * x_one
                g_rows[n] = solved
                x_one, x_two = solved, x_one
            return x_one, x_two

        start = total - span
        state = block(start, span - 1, x_one, x_two)
        finish(start)

        def more(i, state):
            base = total - span * (i + 2)
            state = block(base, span, *state)
            finish(base)
            return state

        lax.fori_loop(0, total // span - 1, more, state)

    pl.semaphore_wait(entered, 3)
    middle = c // blocks

    def to_canal(b, m):
        other = blocks * m + b
        send_tile(send_one.at[b * per + m], recv_one.at[c], (other, k), 0)

    for b in range(blocks):
        halo[2 + 2 * b].wait_recv()
        halo[3 + 2 * b].wait_recv()
        here = slice(b * block, (b + 1) * block)
        for x in range(2):
            fluxes = []
            for v in range(NVAR):
                if x == 0:
                    minus_one = jnp.where(has_last, before[1, v, :, here], 0.0)
                    minus_two = jnp.where(has_last, before[0, v, :, here], 0.0)
                    plus_one = known[1, v, 8:24, here]
                    plus_two = jnp.where(has_next, after[0, v, :, here], 0.0)
                else:
                    minus_one = known[0, v, 8:24, here]
                    minus_two = jnp.where(has_last, before[1, v, :, here], 0.0)
                    plus_one = jnp.where(has_next, after[0, v, :, here], 0.0)
                    plus_two = jnp.where(has_next, after[1, v, :, here], 0.0)
                canal_half = 0.5 * speeds[0, v]
                flux = (canal_half - 0.125) * plus_one - (canal_half + 0.125) * minus_one
                fluxes.append(partial[x, v, :, here] + (flux + (plus_two + minus_two) * (1.0 / 32.0)))
            scale = weight[x, :, here]
            for v in range(NVAR):
                mixed = left[v, 0] * fluxes[0]
                for u in range(1, NVAR):
                    mixed += left[v, u] * fluxes[u]
                rows[x, 16 * v : 16 * v + 16, here] = -(scale * mixed)
            rows[x, 112:128, here] = scale
        pack([rows[x, :, here] for x in range(2)], send_one, b)

        def send_canal(i, carry):
            for sign in (1, -1):
                to_canal(b, lax.rem(middle + sign * (per // 2 - i) + per, per))
            return carry

        to_canal(b, lax.rem(middle + per // 2, per))
        lax.fori_loop(1, per // 2, send_canal, 0)
        mine_now = lax.rem(c, blocks) == b

        @pl.when(mine_now)
        def keep_own():
            pltpu.make_async_copy(
                send_one.at[b * per + middle], recv_one.at[c], recv_sems.at[0]
            ).start()

        @pl.when(jnp.logical_not(mine_now))
        def send_near():
            to_canal(b, middle)

    for b in range(blocks):
        here = slice(b * block, (b + 1) * block)
        pack([jnp.concatenate([weight[x, :, here]] * 8, axis=0) for x in range(2)], vertical_weight, b)
    v_top = lax.rem(sub, 4) == 0
    v_lower, v_centre, v_upper = coefficients(speeds, 2, lane // 16, v_top)

    def v_pick(ref, n, step):
        near, far = ref[n], ref[canals - 1 - n]
        if step:
            near = pltpu.roll(near, 8 - step, 0)
        if step != 2:
            far = pltpu.roll(far, (step + 6) % 8, 0)
        return jnp.where(v_top, near, far)

    def v_factor(m, carry):
        p_one, q_one, p_two, q_two = carry
        for part in range(8):
            n, step = 2 * m + part // 4, part % 4
            w = v_pick(vertical_weight, n, step)
            inverse, multiplier, p_new, q_new = factor(
                w, v_lower, v_centre, v_upper, p_one, q_one, p_two, q_two
            )
            v_inverse[4 * n + step] = inverse
            v_multiplier[4 * n + step] = multiplier
            v_p[4 * n + step] = p_new
            v_q[4 * n + step] = q_new
            p_one, q_one, p_two, q_two = p_new, q_new, p_one, q_one
        return p_one, q_one, p_two, q_two

    lax.fori_loop(0, half // 2, v_factor, (zero, zero, zero, zero))

    wait_for(recv_one, canals, recv_sems.at[0])

    c_lower, c_centre, c_upper = coefficients(speeds, 0, lane // 16, upper_half)
    is_weight = lane >= 112

    def widen(tile):
        w = jnp.where(is_weight, tile, 0.0)
        w += pltpu.roll(w, 16, 1)
        w += pltpu.roll(w, 32, 1)
        return w + pltpu.roll(w, 64, 1)

    def c_forward(i, carry):
        g_one, p_one, q_one, g_two, p_two, q_two = carry
        for m in range(8):
            n = 8 * i + m
            near, far = recv_one[n], recv_one[canals - 1 - n]
            outer = jnp.where(upper_half, near, far)
            inner = pltpu.roll(jnp.where(upper_half, far, near), 4, 0)
            for step, source in enumerate((outer, inner)):
                w = widen(source)
                inverse, multiplier, p_new, q_new = factor(
                    w, c_lower, c_centre, c_upper, p_one, q_one, p_two, q_two
                )
                g_new = (source * inverse - q_new * g_two) - multiplier * g_one
                work_g[2 * n + step] = g_new
                work_p[2 * n + step] = p_new
                work_q[2 * n + step] = q_new
                g_one, p_one, q_one, g_two, p_two, q_two = g_new, p_new, q_new, g_one, p_one, q_one
        return g_one, p_one, q_one, g_two, p_two, q_two

    g_one, p_one, q_one, g_two, p_two, q_two = lax.fori_loop(0, half // 8, c_forward, (zero,) * 6)

    def c_swap(a):
        return pltpu.roll(a, 4, 0)

    x_one = join(c_swap, g_one, g_two, p_one, q_one, p_two, q_two)
    work_g[canals - 1] = x_one

    def c_restore(start):
        for m in range(8):
            n = start // 2 + m
            outer, inner = work_g[start + 2 * m], pltpu.roll(work_g[start + 2 * m + 1], 4, 0)
            for pair, tile in (
                (n, jnp.where(upper_half, outer, inner)),
                (canals - 1 - n, jnp.where(upper_half, inner, outer)),
            ):
                group, place = partner_of(pair, c, crosses)
                send_two[group * places + place] = jnp.where(is_weight, recv_one[pair], tile)

    retreat(work_p, work_q, work_g, canals, 16, x_one, c_swap(x_one), c_restore)

    def group_of(ref, position):
        return ref.at[pl.ds(position * places, places)]

    def send_cross(i, carry):
        other = lax.rem(k + i, crosses)
        send_tile(group_of(send_two, other), group_of(recv_two, k), (c, other), 1)
        return carry

    lax.fori_loop(1, crosses, send_cross, 0)
    pltpu.make_async_copy(group_of(send_two, k), group_of(recv_two, k), recv_sems.at[1]).start()
    wait_for(recv_two, canals, recv_sems.at[1])

    count = crosses // 2
    lines = 8 * places
    for pair in range(count):
        near = recv_two[pair * places : (pair + 1) * places].reshape(lines, 128)
        other = crosses - 1 - pair
        far = recv_two[other * places : (other + 1) * places].reshape(lines, 128)
        turned[pair] = jnp.concatenate([near, far], axis=0).T

    x_top = lane < lines
    x_lower, x_centre, x_upper = coefficients(speeds, 1, sub, x_top)

    def x_forward(pair, carry):
        g_one, p_one, q_one, g_two, p_two, q_two = carry
        for y in range(16):
            source = jnp.where(
                x_top,
                turned[pair, pl.ds(y, 8, stride=16), :],
                turned[pair, pl.ds(15 - y, 8, stride=16), :],
            )
            w = jnp.broadcast_to(source[7:8], TILE)
            inverse, multiplier, p_new, q_new = factor(
                w, x_lower, x_centre, x_upper, p_one, q_one, p_two, q_two
            )
            g_new = (source * inverse - q_new * g_two) - multiplier * g_one
            work_g[16 * pair + y] = g_new
            work_p[16 * pair + y] = p_new
            work_q[16 * pair + y] = q_new
            g_one, p_one, q_one, g_two, p_two, q_two = g_new, p_new, q_new, g_one, p_one, q_one
        return g_one, p_one, q_one, g_two, p_two, q_two

    g_one, p_one, q_one, g_two, p_two, q_two = lax.fori_loop(0, count, x_forward, (zero,) * 6)

    def x_swap(a):
        return pltpu.roll(a, lines, 1)

    x_one = join(x_swap, g_one, g_two, p_one, q_one, p_two, q_two)
    work_g[16 * count - 1] = x_one

    chunk_here = c // blocks + per * lax.rem(c, blocks)

    def send_home(pair):
        def one(i, carry):
            place = lax.rem(i + c, places)
            target = pair_of(k, c, place, crosses)
            for other in (pair, crosses - 1 - pair):
                source = send_three.at[other * places + place]
                itself = jnp.logical_and(target == c, other == k)

                @pl.when(itself)
                def keep():
                    pltpu.make_async_copy(source, recv_three.at[chunk_here], recv_sems.at[2]).start()

                @pl.when(jnp.logical_not(itself))
                def send():
                    send_tile(source, recv_three.at[chunk_here], (target, other), 2)

            return carry

        lax.fori_loop(0, places, one, 0)

    diagonal = lane // 16 == sub

    def fold(tile):
        last_row = jnp.where(diagonal, jnp.broadcast_to(tile[7:8], TILE), 0.0)
        last_row += pltpu.roll(last_row, 16, 1)
        last_row += pltpu.roll(last_row, 32, 1)
        last_row += pltpu.roll(last_row, 64, 1)
        return jnp.where(is_weight, last_row, tile)[0:7]

    def x_restore(start):
        pair = start // 16
        for y in range(16):
            turned[pair, pl.ds(y, 8, stride=16), :] = jnp.where(
                x_top, work_g[start + y], work_g[start + 15 - y]
            )
        back = turned[pair].T
        for block in range(places):
            at = 8 * block
            send_three[pair * places + block] = fold(back[at : at + 8])
            send_three[(crosses - 1 - pair) * places + block] = fold(back[lines + at : lines + at + 8])
        send_home(pair)

    retreat(work_p, work_q, work_g, 16 * count, 16, x_one, x_swap(x_one), x_restore)
    wait_for(recv_three, canals, recv_sems.at[2])

    def unfold(i, carry):
        for m in range(8):
            n = 8 * i + m
            home[n, 0:7] = recv_three[n]
            free = jnp.where(is_weight[0:7], recv_three[n], 0.0)
            free += pltpu.roll(free, 16, 1)
            free += pltpu.roll(free, 32, 1)
            free += pltpu.roll(free, 64, 1)
            home[n, 7:8] = jnp.sum(jnp.where(diagonal[0:7], free, 0.0), axis=0, keepdims=True)
        return carry

    lax.fori_loop(0, canals // 8, unfold, 0)

    def v_forward(m, carry):
        g_one, g_two = carry
        for step in range(16):
            i = 16 * m + step
            source = v_pick(home, 4 * m + step // 4, step % 4)
            g_new = (source * v_inverse[i] - v_q[i] * g_two) - v_multiplier[i] * g_one
            v_g[i] = g_new
            g_one, g_two = g_new, g_one
        return g_one, g_two

    g_one, g_two = lax.fori_loop(0, half // 4, v_forward, (zero, zero))

    def v_swap(a):
        return jnp.where(v_top, pltpu.roll(a, 7, 0), pltpu.roll(a, 1, 0))

    last = 2 * canals - 1
    x_one = join(v_swap, g_one, g_two, v_p[last], v_q[last], v_p[last - 1], v_q[last - 1])
    v_g[last] = x_one

    place_of = lax.rem(sub, 4)

    def v_chunk(n):
        near, far = [], []
        for part in range(2):
            base = 8 * n + 4 * part
            near_tile = v_g[base]
            far_tile = pltpu.roll(v_g[base], 2, 0)
            for step in range(1, 4):
                near_tile = jnp.where(
                    place_of == step, pltpu.roll(v_g[base + step], step, 0), near_tile
                )
                far_tile = jnp.where(
                    place_of == 3 - step,
                    pltpu.roll(v_g[base + step], (10 - step) % 8, 0),
                    far_tile,
                )
            near.append(near_tile)
            far.append(far_tile)
        far = far[::-1]
        at = pl.multiple_of(8 * n, 8)
        end = pl.multiple_of(depth - 8 - 8 * n, 8)
        for start, (one, two) in ((at, near), (end, far)):
            upright[0, pl.ds(start, 8), :] = jnp.where(upper_half, one, pltpu.roll(two, 4, 0))
            upright[1, pl.ds(start, 8), :] = jnp.where(upper_half, pltpu.roll(one, 4, 0), two)

    def v_restore(start):
        v_chunk(start // 8)
        v_chunk(start // 8 + 1)

    retreat(v_p, v_q, v_g, 2 * canals, 16, x_one, v_swap(x_one), v_restore)

    for x in range(2):
        for b in range(blocks):
            third = upright[x, b * block : (b + 1) * block, :].T
            for v in range(NVAR):
                mixed = right[v, 0] * third[0:16]
                for u in range(1, NVAR):
                    mixed += right[v, u] * third[16 * u : 16 * u + 16]
                update[x, v, :, b * block : (b + 1) * block] = mixed

    for copy in halo:
        copy.wait_send()
    wait_for(send_one, canals - 1, send_sems.at[0])
    wait_for(send_two, canals - places, send_sems.at[1])
    mine, unused = partner_of(c, c, crosses)

    @pl.when(mine == k)
    def sent_fewer():
        wait_for(send_three, canals - 1, send_sems.at[2])

    @pl.when(mine != k)
    def sent_all():
        wait_for(send_three, canals, send_sems.at[2])


def solution(mesh):
    canals, crosses = mesh.shape["canal"], mesh.shape["cross"]
    depth = 4 * canals
    cells = (2, NVAR, 16, depth)
    tiles = (canals,) + TILE
    transfers = 2 + 2 * (depth // min(depth, 128))

    def shards(conserved, iblank, step_scale, speeds, left_vectors, right_vectors):
        vmem = pl.BlockSpec(memory_space=pltpu.VMEM)
        anywhere = pl.BlockSpec(memory_space=pl.ANY)

        def held(*shape):
            return pltpu.VMEM(shape, F32)

        return pl.pallas_call(
            functools.partial(kernel, canals, crosses),
            out_shape=jax.ShapeDtypeStruct(cells, F32),
            in_specs=[anywhere] * 6,
            out_specs=vmem,
            scratch_shapes=[
                held(*cells),
                pltpu.VMEM((2, 16, depth), jnp.int32),
                held(2, 16, depth),
                pltpu.SMEM((3, NVAR), F32),
                pltpu.SMEM((NVAR, NVAR), F32),
                pltpu.SMEM((NVAR, NVAR), F32),
                held(2, NVAR, 32, depth),
                held(2, 16, depth),
                held(2, NVAR, 2, depth),
                held(2, NVAR, 2, depth),
                held(2, NVAR, 2, depth),
                held(2, NVAR, 2, depth),
                held(*cells),
                held(*cells),
                held(*cells),
                held(2, 128, depth),
                held(*tiles),
                held(*tiles),
                held(*tiles),
                held(*tiles),
                held(crosses // 2, 128, 16 * (canals // crosses)),
                held(canals, 7, 128),
                held(canals, 7, 128),
                held(*tiles),
                held(*tiles),
                held(2, depth, 128),
                held(2 * canals, *TILE),
                held(2 * canals, *TILE),
                held(2 * canals, *TILE),
                held(2 * canals, *TILE),
                held(max(canals, 8 * crosses), *TILE),
                held(max(canals, 8 * crosses), *TILE),
                held(max(canals, 8 * crosses), *TILE),
                held(2 * canals, *TILE),
                pltpu.SemaphoreType.DMA((6,)),
                pltpu.SemaphoreType.DMA((transfers,)),
                pltpu.SemaphoreType.DMA((transfers,)),
                pltpu.SemaphoreType.DMA((3,)),
                pltpu.SemaphoreType.DMA((3,)),
                pltpu.SemaphoreType.REGULAR,
            ],
            compiler_params=pltpu.CompilerParams(
                collective_id=0, has_side_effects=True, vmem_limit_bytes=60 * 1024 * 1024
            ),
        )(conserved, iblank, step_scale, speeds, left_vectors, right_vectors)

    return jax.shard_map(
        shards,
        mesh=mesh,
        in_specs=(
            P("canal", None, "cross", None),
            P("canal", "cross", None),
            P("canal", "cross", None),
            P(),
            P(),
            P(),
        ),
        out_specs=P("canal", None, "cross", None),
        check_vma=False,
    )
```

```python
import functools

import jax
import jax.numpy as jnp
from jax import lax
from jax.experimental import pallas as pl
from jax.experimental.pallas import tpu as pltpu
from jax.sharding import PartitionSpec as P

MESH = pl.DeviceIdType.MESH
F32 = jnp.float32
NVAR = 7
TILE = (8, 128)


def turn_of(canal, crosses):
    return lax.rem(canal // 4, crosses)


def partner_of(pair, canal, crosses):
    return lax.rem(lax.rem(pair, crosses) + turn_of(canal, crosses), crosses), pair // crosses


def pair_of(group, canal, place, crosses):
    return crosses * place + lax.rem(group - turn_of(canal, crosses) + crosses, crosses)


def factor(w, lower, centre, upper, p_one, q_one, p_two, q_two):
    damping = 0.25 * w
    reduced = w * (0.25 * p_two - lower)
    pivot = (1.0 + centre * w + damping * q_two) - reduced * p_one
    inverse = 1.0 / pivot
    q_new = -damping * inverse
    p_new = -(upper * w + reduced * q_one) * inverse
    return inverse, reduced * inverse, p_new, q_new


def join(swap, g_one, g_two, p_one, q_one, p_two, q_two):
    alpha = 1.0 - q_one * swap(q_two)
    beta = p_one - q_one * swap(p_two)
    gamma = g_one - q_one * swap(g_two)
    alpha_far, beta_far, gamma_far = swap(alpha), swap(beta), swap(gamma)
    return (gamma * alpha_far - beta * gamma_far) / (alpha * alpha_far - beta * beta_far)


def spread(speeds_ref, direction, index):
    forward = jnp.zeros(index.shape, F32)
    backward = jnp.zeros(index.shape, F32)
    for v in range(NVAR):
        speed = speeds_ref[direction, v]
        forward = jnp.where(index == v, jnp.maximum(speed, 0.0), forward)
        backward = jnp.where(index == v, jnp.maximum(-speed, 0.0), backward)
    return forward, backward


def coefficients(speeds_ref, direction, index, top):
    forward, backward = spread(speeds_ref, direction, index)
    lower = jnp.where(top, forward, backward) + 0.25
    upper = jnp.where(top, backward, forward) + 0.25
    return lower, 1.0 + forward + backward, upper


def kernel(
    canals,
    crosses,
    conserved_hbm,
    iblank_hbm,
    step_scale_hbm,
    speeds_hbm,
    left_hbm,
    right_hbm,
    update,
    conserved,
    iblank,
    step_scale,
    speeds,
    left,
    right,
    known,
    weight,
    low_out,
    high_out,
    low_in,
    high_in,
    before,
    after,
    partial,
    rows,
    send_one,
    recv_one,
    send_two,
    recv_two,
    turned,
    send_three,
    recv_three,
    vertical_weight,
    upright,
    result,
    v_inverse,
    v_multiplier,
    v_p,
    v_q,
    work_p,
    work_q,
    work_g,
    v_g,
    load_sems,
    halo_send,
    halo_recv,
    send_sems,
    recv_sems,
    out_sems,
    entered,
):
    depth = 4 * canals
    block = min(depth, 128)
    blocks = depth // block
    places = canals // crosses
    half = canals // 2
    per = canals // blocks
    c = lax.axis_index("canal")
    k = lax.axis_index("cross")

    loads = [
        pltpu.make_async_copy(source, target, load_sems.at[number])
        for number, (source, target) in enumerate(
            (
                (iblank_hbm, iblank),
                (conserved_hbm, conserved),
                (step_scale_hbm, step_scale),
                (speeds_hbm, speeds),
                (left_hbm, left),
                (right_hbm, right),
            )
        )
    ]
    for load in loads:
        load.start()

    barrier = pltpu.get_barrier_semaphore()
    c_next, c_last = lax.rem(c + 1, canals), lax.rem(c + canals - 1, canals)
    k_next, k_last = lax.rem(k + 1, crosses), lax.rem(k + crosses - 1, crosses)

    def greet(device):
        pl.semaphore_signal(barrier, inc=1, device_id=device, device_id_type=MESH)

    def row_mate(i):
        return 4 * (c // 4) + lax.rem(c + i, 4)

    greet((c_next, k))
    greet((c_last, k))
    for i in range(1, canals // 4):
        greet((lax.rem(c + 4 * i, canals), k))
    for i in range(1, crosses):
        greet((c, lax.rem(k + i, crosses)))
    for i in range(1, 4):
        greet((row_mate(i), k))
    for load in loads:
        load.wait()

    for x in range(2):
        flag = iblank[x]
        live = (flag != 0).astype(F32)
        weight[x] = jnp.where(flag == 1, step_scale[x], 0.0)
        for v in range(NVAR):
            cells = conserved[x, v] * live
            known[x, v, 8:24, :] = cells
            low_out[x, v] = cells[0:2]
            high_out[x, v] = cells[14:16]

    pl.semaphore_wait(barrier, 2 + canals // 4 - 1 + crosses - 1 + 3)

    def lanes(ref, b):
        return ref.at[:, :, :, pl.ds(b * block, block)]

    transfers = [(high_out, low_in, (c, k_next)), (low_out, high_in, (c, k_last))]
    for b in range(blocks):
        own = known.at[:, :, pl.ds(8, 16), pl.ds(b * block, block)]
        transfers.append((own, lanes(before, b), (c_next, k)))
        transfers.append((own, lanes(after, b), (c_last, k)))
    halo = []
    for number, (source, target, device) in enumerate(transfers):
        copy = pltpu.make_async_remote_copy(
            src_ref=source,
            dst_ref=target,
            send_sem=halo_send.at[number],
            recv_sem=halo_recv.at[number],
            device_id=device,
            device_id_type=MESH,
        )
        copy.start()
        halo.append(copy)

    for i in range(1, 4):
        pl.semaphore_signal(entered, inc=1, device_id=(row_mate(i), k), device_id_type=MESH)

    lane = lax.broadcasted_iota(jnp.int32, TILE, 1)
    sub = lax.broadcasted_iota(jnp.int32, TILE, 0)
    upper_half = sub < 4
    zero = jnp.zeros(TILE, F32)

    def pack(matrices, target, b):
        first, second = matrices[0].T, matrices[1].T
        for n in range(block // 8):
            one, two = first[8 * n : 8 * n + 8], second[8 * n : 8 * n + 8]
            chunk = b * per + 2 * n
            target[chunk] = jnp.where(upper_half, one, pltpu.roll(two, 4, 0))
            target[chunk + 1] = jnp.where(upper_half, pltpu.roll(one, 4, 0), two)

    halo[0].wait_recv()
    halo[1].wait_recv()
    has_last, has_next = c > 0, c < canals - 1
    low_mask, high_mask = k > 0, k < crosses - 1
    zi = lax.broadcasted_iota(jnp.int32, (16, depth), 1)
    for x in range(2):
        for v in range(NVAR):
            known[x, v, 6:8, :] = jnp.where(low_mask, low_in[x, v], 0.0)
            known[x, v, 24:26, :] = jnp.where(high_mask, high_in[x, v], 0.0)
            here = known[x, v, 8:24, :]
            z_half = 0.5 * speeds[2, v]
            up_one = jnp.where(zi < depth - 1, pltpu.roll(here, depth - 1, 1), 0.0)
            up_two = jnp.where(zi < depth - 2, pltpu.roll(here, depth - 2, 1), 0.0)
            down_one = jnp.where(zi >= 1, pltpu.roll(here, 1, 1), 0.0)
            down_two = jnp.where(zi >= 2, pltpu.roll(here, 2, 1), 0.0)
            flux = (z_half - 0.125) * up_one - (z_half + 0.125) * down_one
            outer = up_two + down_two
            cross_half = 0.5 * speeds[1, v]
            flux += (cross_half - 0.125) * known[x, v, 9:25, :]
            flux -= (cross_half + 0.125) * known[x, v, 7:23, :]
            outer += known[x, v, 10:26, :] + known[x, v, 6:22, :]
            partial[x, v] = flux + (outer + 18.0 * here) * (1.0 / 32.0)

    def send_tile(source, target, device, number):
        pltpu.make_async_remote_copy(
            src_ref=source,
            dst_ref=target,
            send_sem=send_sems.at[number],
            recv_sem=recv_sems.at[number],
            device_id=device,
            device_id_type=MESH,
        ).start()

    def wait_for(ref, count, sem):
        part = ref.at[pl.ds(0, count)]
        pltpu.make_async_copy(part, part, sem).wait()

    def retreat(p_rows, q_rows, g_rows, total, span, x_one, x_two, finish):
        def block(base, length, x_one, x_two):
            for i in range(length - 1, -1, -1):
                n = base + i
                solved = (g_rows[n] - q_rows[n] * x_two) - p_rows[n] * x_one
                g_rows[n] = solved
                x_one, x_two = solved, x_one
            return x_one, x_two

        start = total - span
        state = block(start, span - 1, x_one, x_two)
        finish(start)

        def more(i, state):
            base = total - span * (i + 2)
            state = block(base, span, *state)
            finish(base)
            return state

        lax.fori_loop(0, total // span - 1, more, state)

    pl.semaphore_wait(entered, 3)
    middle = c // blocks

    def to_canal(b, m):
        other = blocks * m + b
        send_tile(send_one.at[b * per + m], recv_one.at[c], (other, k), 0)

    for b in range(blocks):
        halo[2 + 2 * b].wait_recv()
        halo[3 + 2 * b].wait_recv()
        here = slice(b * block, (b + 1) * block)
        for x in range(2):
            fluxes = []
            for v in range(NVAR):
                if x == 0:
                    minus_one = jnp.where(has_last, before[1, v, :, here], 0.0)
                    minus_two = jnp.where(has_last, before[0, v, :, here], 0.0)
                    plus_one = known[1, v, 8:24, here]
                    plus_two = jnp.where(has_next, after[0, v, :, here], 0.0)
                else:
                    minus_one = known[0, v, 8:24, here]
                    minus_two = jnp.where(has_last, before[1, v, :, here], 0.0)
                    plus_one = jnp.where(has_next, after[0, v, :, here], 0.0)
                    plus_two = jnp.where(has_next, after[1, v, :, here], 0.0)
                canal_half = 0.5 * speeds[0, v]
                flux = (canal_half - 0.125) * plus_one - (canal_half + 0.125) * minus_one
                fluxes.append(partial[x, v, :, here] + (flux + (plus_two + minus_two) * (1.0 / 32.0)))
            scale = weight[x, :, here]
            for v in range(NVAR):
                mixed = left[v, 0] * fluxes[0]
                for u in range(1, NVAR):
                    mixed += left[v, u] * fluxes[u]
                rows[x, 16 * v : 16 * v + 16, here] = -(scale * mixed)
            rows[x, 112:128, here] = scale
        pack([rows[x, :, here] for x in range(2)], send_one, b)

        def send_canal(i, carry):
            for sign in (1, -1):
                to_canal(b, lax.rem(middle + sign * (per // 2 - i) + per, per))
            return carry

        to_canal(b, lax.rem(middle + per // 2, per))
        lax.fori_loop(1, per // 2, send_canal, 0)
        mine_now = lax.rem(c, blocks) == b

        @pl.when(mine_now)
        def keep_own():
            pltpu.make_async_copy(
                send_one.at[b * per + middle], recv_one.at[c], recv_sems.at[0]
            ).start()

        @pl.when(jnp.logical_not(mine_now))
        def send_near():
            to_canal(b, middle)

    for b in range(blocks):
        here = slice(b * block, (b + 1) * block)
        pack([jnp.concatenate([weight[x, :, here]] * 8, axis=0) for x in range(2)], vertical_weight, b)
    v_top = lax.rem(sub, 4) == 0
    v_lower, v_centre, v_upper = coefficients(speeds, 2, lane // 16, v_top)

    def v_pick(ref, n, step):
        near, far = ref[n], ref[canals - 1 - n]
        if step:
            near = pltpu.roll(near, 8 - step, 0)
        if step != 2:
            far = pltpu.roll(far, (step + 6) % 8, 0)
        return jnp.where(v_top, near, far)

    def v_factor(m, carry):
        p_one, q_one, p_two, q_two = carry
        for part in range(8):
            n, step = 2 * m + part // 4, part % 4
            w = v_pick(vertical_weight, n, step)
            inverse, multiplier, p_new, q_new = factor(
                w, v_lower, v_centre, v_upper, p_one, q_one, p_two, q_two
            )
            v_inverse[4 * n + step] = inverse
            v_multiplier[4 * n + step] = multiplier
            v_p[4 * n + step] = p_new
            v_q[4 * n + step] = q_new
            p_one, q_one, p_two, q_two = p_new, q_new, p_one, q_one
        return p_one, q_one, p_two, q_two

    lax.fori_loop(0, half // 2, v_factor, (zero, zero, zero, zero))

    wait_for(recv_one, canals, recv_sems.at[0])

    c_lower, c_centre, c_upper = coefficients(speeds, 0, lane // 16, upper_half)
    is_weight = lane >= 112

    def widen(tile):
        w = jnp.where(is_weight, tile, 0.0)
        w += pltpu.roll(w, 16, 1)
        w += pltpu.roll(w, 32, 1)
        return w + pltpu.roll(w, 64, 1)

    def c_forward(i, carry):
        g_one, p_one, q_one, g_two, p_two, q_two = carry
        for m in range(8):
            n = 8 * i + m
            near, far = recv_one[n], recv_one[canals - 1 - n]
            outer = jnp.where(upper_half, near, far)
            inner = pltpu.roll(jnp.where(upper_half, far, near), 4, 0)
            for step, source in enumerate((outer, inner)):
                w = widen(source)
                inverse, multiplier, p_new, q_new = factor(
                    w, c_lower, c_centre, c_upper, p_one, q_one, p_two, q_two
                )
                g_new = (source * inverse - q_new * g_two) - multiplier * g_one
                work_g[2 * n + step] = g_new
                work_p[2 * n + step] = p_new
                work_q[2 * n + step] = q_new
                g_one, p_one, q_one, g_two, p_two, q_two = g_new, p_new, q_new, g_one, p_one, q_one
        return g_one, p_one, q_one, g_two, p_two, q_two

    g_one, p_one, q_one, g_two, p_two, q_two = lax.fori_loop(0, half // 8, c_forward, (zero,) * 6)

    def c_swap(a):
        return pltpu.roll(a, 4, 0)

    x_one = join(c_swap, g_one, g_two, p_one, q_one, p_two, q_two)
    work_g[canals - 1] = x_one

    def c_restore(start):
        for m in range(8):
            n = start // 2 + m
            outer, inner = work_g[start + 2 * m], pltpu.roll(work_g[start + 2 * m + 1], 4, 0)
            for pair, tile in (
                (n, jnp.where(upper_half, outer, inner)),
                (canals - 1 - n, jnp.where(upper_half, inner, outer)),
            ):
                group, place = partner_of(pair, c, crosses)
                send_two[group * places + place] = jnp.where(is_weight, recv_one[pair], tile)

    retreat(work_p, work_q, work_g, canals, 16, x_one, c_swap(x_one), c_restore)

    def group_of(ref, position):
        return ref.at[pl.ds(position * places, places)]

    def send_cross(i, carry):
        other = lax.rem(k + i, crosses)
        send_tile(group_of(send_two, other), group_of(recv_two, k), (c, other), 1)
        return carry

    lax.fori_loop(1, crosses, send_cross, 0)
    pltpu.make_async_copy(group_of(send_two, k), group_of(recv_two, k), recv_sems.at[1]).start()
    wait_for(recv_two, canals, recv_sems.at[1])

    count = crosses // 2
    lines = 8 * places
    for pair in range(count):
        near = recv_two[pair * places : (pair + 1) * places].reshape(lines, 128)
        other = crosses - 1 - pair
        far = recv_two[other * places : (other + 1) * places].reshape(lines, 128)
        turned[pair] = jnp.concatenate([near, far], axis=0).T

    x_top = lane < lines
    x_lower, x_centre, x_upper = coefficients(speeds, 1, sub, x_top)

    def x_forward(pair, carry):
        g_one, p_one, q_one, g_two, p_two, q_two = carry
        for y in range(16):
            source = jnp.where(
                x_top,
                turned[pair, pl.ds(y, 8, stride=16), :],
                turned[pair, pl.ds(15 - y, 8, stride=16), :],
            )
            w = jnp.broadcast_to(source[7:8], TILE)
            inverse, multiplier, p_new, q_new = factor(
                w, x_lower, x_centre, x_upper, p_one, q_one, p_two, q_two
            )
            g_new = (source * inverse - q_new * g_two) - multiplier * g_one
            work_g[16 * pair + y] = g_new
            work_p[16 * pair + y] = p_new
            work_q[16 * pair + y] = q_new
            g_one, p_one, q_one, g_two, p_two, q_two = g_new, p_new, q_new, g_one, p_one, q_one
        return g_one, p_one, q_one, g_two, p_two, q_two

    g_one, p_one, q_one, g_two, p_two, q_two = lax.fori_loop(0, count, x_forward, (zero,) * 6)

    def x_swap(a):
        return pltpu.roll(a, lines, 1)

    x_one = join(x_swap, g_one, g_two, p_one, q_one, p_two, q_two)
    work_g[16 * count - 1] = x_one

    chunk_here = c // blocks + per * lax.rem(c, blocks)

    def send_home(pair):
        def one(i, carry):
            place = lax.rem(i + c, places)
            target = pair_of(k, c, place, crosses)
            for other in (pair, crosses - 1 - pair):
                source = send_three.at[other * places + place]
                itself = jnp.logical_and(target == c, other == k)

                @pl.when(itself)
                def keep():
                    pltpu.make_async_copy(source, recv_three.at[chunk_here], recv_sems.at[2]).start()

                @pl.when(jnp.logical_not(itself))
                def send():
                    send_tile(source, recv_three.at[chunk_here], (target, other), 2)

            return carry

        lax.fori_loop(0, places, one, 0)

    def x_restore(start):
        pair = start // 16
        for y in range(16):
            turned[pair, pl.ds(y, 8, stride=16), :] = jnp.where(
                x_top, work_g[start + y], work_g[start + 15 - y]
            )
        back = turned[pair].T
        for block in range(places):
            at = 8 * block
            send_three[pair * places + block] = back[at : at + 8]
            send_three[(crosses - 1 - pair) * places + block] = back[lines + at : lines + at + 8]
        send_home(pair)

    retreat(work_p, work_q, work_g, 16 * count, 16, x_one, x_swap(x_one), x_restore)
    wait_for(recv_three, canals, recv_sems.at[2])

    def v_forward(m, carry):
        g_one, g_two = carry
        for step in range(16):
            i = 16 * m + step
            source = v_pick(recv_three, 4 * m + step // 4, step % 4)
            g_new = (source * v_inverse[i] - v_q[i] * g_two) - v_multiplier[i] * g_one
            v_g[i] = g_new
            g_one, g_two = g_new, g_one
        return g_one, g_two

    g_one, g_two = lax.fori_loop(0, half // 4, v_forward, (zero, zero))

    def v_swap(a):
        return jnp.where(v_top, pltpu.roll(a, 7, 0), pltpu.roll(a, 1, 0))

    last = 2 * canals - 1
    x_one = join(v_swap, g_one, g_two, v_p[last], v_q[last], v_p[last - 1], v_q[last - 1])
    v_g[last] = x_one

    place_of = lax.rem(sub, 4)

    def v_chunk(n):
        near, far = [], []
        for part in range(2):
            base = 8 * n + 4 * part
            near_tile = v_g[base]
            far_tile = pltpu.roll(v_g[base], 2, 0)
            for step in range(1, 4):
                near_tile = jnp.where(
                    place_of == step, pltpu.roll(v_g[base + step], step, 0), near_tile
                )
                far_tile = jnp.where(
                    place_of == 3 - step,
                    pltpu.roll(v_g[base + step], (10 - step) % 8, 0),
                    far_tile,
                )
            near.append(near_tile)
            far.append(far_tile)
        far = far[::-1]
        at = pl.multiple_of(8 * n, 8)
        end = pl.multiple_of(depth - 8 - 8 * n, 8)
        for start, (one, two) in ((at, near), (end, far)):
            upright[0, pl.ds(start, 8), :] = jnp.where(upper_half, one, pltpu.roll(two, 4, 0))
            upright[1, pl.ds(start, 8), :] = jnp.where(upper_half, pltpu.roll(one, 4, 0), two)

    def v_restore(start):
        v_chunk(start // 8)
        v_chunk(start // 8 + 1)

    retreat(v_p, v_q, v_g, 2 * canals, 16, x_one, v_swap(x_one), v_restore)

    outgoing = []
    for x in range(2):
        for b in range(blocks):
            third = upright[x, b * block : (b + 1) * block, :].T
            for v in range(NVAR):
                mixed = right[v, 0] * third[0:16]
                for u in range(1, NVAR):
                    mixed += right[v, u] * third[16 * u : 16 * u + 16]
                result[x, v, :, b * block : (b + 1) * block] = mixed
            finished = pltpu.make_async_copy(
                result.at[x, :, :, pl.ds(b * block, block)],
                update.at[x, :, :, pl.ds(b * block, block)],
                out_sems.at[x * blocks + b],
            )
            finished.start()
            outgoing.append(finished)

    for copy in halo:
        copy.wait_send()
    wait_for(send_one, canals - 1, send_sems.at[0])
    wait_for(send_two, canals - places, send_sems.at[1])
    mine, unused = partner_of(c, c, crosses)

    @pl.when(mine == k)
    def sent_fewer():
        wait_for(send_three, canals - 1, send_sems.at[2])

    @pl.when(mine != k)
    def sent_all():
        wait_for(send_three, canals, send_sems.at[2])

    for finished in outgoing:
        finished.wait()


def solution(mesh):
    canals, crosses = mesh.shape["canal"], mesh.shape["cross"]
    depth = 4 * canals
    cells = (2, NVAR, 16, depth)
    tiles = (canals,) + TILE
    transfers = 2 + 2 * (depth // min(depth, 128))

    def shards(conserved, iblank, step_scale, speeds, left_vectors, right_vectors):
        anywhere = pl.BlockSpec(memory_space=pl.ANY)

        def held(*shape):
            return pltpu.VMEM(shape, F32)

        return pl.pallas_call(
            functools.partial(kernel, canals, crosses),
            out_shape=jax.ShapeDtypeStruct(cells, F32),
            in_specs=[anywhere] * 6,
            out_specs=anywhere,
            scratch_shapes=[
                held(*cells),
                pltpu.VMEM((2, 16, depth), jnp.int32),
                held(2, 16, depth),
                pltpu.SMEM((3, NVAR), F32),
                pltpu.SMEM((NVAR, NVAR), F32),
                pltpu.SMEM((NVAR, NVAR), F32),
                held(2, NVAR, 32, depth),
                held(2, 16, depth),
                held(2, NVAR, 2, depth),
                held(2, NVAR, 2, depth),
                held(2, NVAR, 2, depth),
                held(2, NVAR, 2, depth),
                held(*cells),
                held(*cells),
                held(*cells),
                held(2, 128, depth),
                held(*tiles),
                held(*tiles),
                held(*tiles),
                held(*tiles),
                held(crosses // 2, 128, 16 * (canals // crosses)),
                held(*tiles),
                held(*tiles),
                held(*tiles),
                held(2, depth, 128),
                held(*cells),
                held(2 * canals, *TILE),
                held(2 * canals, *TILE),
                held(2 * canals, *TILE),
                held(2 * canals, *TILE),
                held(max(canals, 8 * crosses), *TILE),
                held(max(canals, 8 * crosses), *TILE),
                held(max(canals, 8 * crosses), *TILE),
                held(2 * canals, *TILE),
                pltpu.SemaphoreType.DMA((6,)),
                pltpu.SemaphoreType.DMA((transfers,)),
                pltpu.SemaphoreType.DMA((transfers,)),
                pltpu.SemaphoreType.DMA((3,)),
                pltpu.SemaphoreType.DMA((3,)),
                pltpu.SemaphoreType.DMA((transfers - 2,)),
                pltpu.SemaphoreType.REGULAR,
            ],
            compiler_params=pltpu.CompilerParams(
                collective_id=0, has_side_effects=True, vmem_limit_bytes=60 * 1024 * 1024
            ),
        )(conserved, iblank, step_scale, speeds, left_vectors, right_vectors)

    return jax.shard_map(
        shards,
        mesh=mesh,
        in_specs=(
            P("canal", None, "cross", None),
            P("canal", "cross", None),
            P("canal", "cross", None),
            P(),
            P(),
            P(),
        ),
        out_specs=P("canal", None, "cross", None),
        check_vma=False,
    )
```

```python
import functools

import jax
import jax.numpy as jnp
from jax import lax
from jax.experimental import pallas as pl
from jax.experimental.pallas import tpu as pltpu
from jax.sharding import PartitionSpec as P

MESH = pl.DeviceIdType.MESH
F32 = jnp.float32
NVAR = 7
TILE = (8, 128)


def turn_of(canal, crosses):
    return lax.rem(canal // 4, crosses)


def partner_of(pair, canal, crosses):
    return lax.rem(lax.rem(pair, crosses) + turn_of(canal, crosses), crosses), pair // crosses


def pair_of(group, canal, place, crosses):
    return crosses * place + lax.rem(group - turn_of(canal, crosses) + crosses, crosses)


def factor(w, lower, centre, upper, p_one, q_one, p_two, q_two):
    damping = 0.25 * w
    reduced = w * (0.25 * p_two - lower)
    pivot = (1.0 + centre * w + damping * q_two) - reduced * p_one
    inverse = 1.0 / pivot
    q_new = -damping * inverse
    p_new = -(upper * w + reduced * q_one) * inverse
    return inverse, reduced * inverse, p_new, q_new


def join(swap, g_one, g_two, p_one, q_one, p_two, q_two):
    alpha = 1.0 - q_one * swap(q_two)
    beta = p_one - q_one * swap(p_two)
    gamma = g_one - q_one * swap(g_two)
    alpha_far, beta_far, gamma_far = swap(alpha), swap(beta), swap(gamma)
    return (gamma * alpha_far - beta * gamma_far) / (alpha * alpha_far - beta * beta_far)


def spread(speeds_ref, direction, index):
    forward = jnp.zeros(index.shape, F32)
    backward = jnp.zeros(index.shape, F32)
    for v in range(NVAR):
        speed = speeds_ref[direction, v]
        forward = jnp.where(index == v, jnp.maximum(speed, 0.0), forward)
        backward = jnp.where(index == v, jnp.maximum(-speed, 0.0), backward)
    return forward, backward


def coefficients(speeds_ref, direction, index, top):
    forward, backward = spread(speeds_ref, direction, index)
    lower = jnp.where(top, forward, backward) + 0.25
    upper = jnp.where(top, backward, forward) + 0.25
    return lower, 1.0 + forward + backward, upper


def kernel(
    canals,
    crosses,
    conserved_hbm,
    iblank_hbm,
    step_scale_hbm,
    speeds_hbm,
    left_hbm,
    right_hbm,
    update,
    conserved,
    iblank,
    step_scale,
    speeds,
    left,
    right,
    known,
    weight,
    low_out,
    high_out,
    low_in,
    high_in,
    before,
    after,
    partial,
    rows,
    send_one,
    recv_one,
    send_two,
    recv_two,
    turned,
    send_three,
    recv_three,
    vertical_weight,
    upright,
    result,
    v_inverse,
    v_multiplier,
    v_p,
    v_q,
    work_p,
    work_q,
    work_g,
    v_g,
    load_sems,
    halo_send,
    halo_recv,
    send_sems,
    recv_sems,
    out_sems,
    entered,
):
    depth = 4 * canals
    block = min(depth, 128)
    blocks = depth // block
    places = canals // crosses
    half = canals // 2
    per = canals // blocks
    c = lax.axis_index("canal")
    k = lax.axis_index("cross")

    loads = [
        pltpu.make_async_copy(source, target, load_sems.at[number])
        for number, (source, target) in enumerate(
            (
                (iblank_hbm, iblank),
                (conserved_hbm, conserved),
                (step_scale_hbm, step_scale),
                (speeds_hbm, speeds),
                (left_hbm, left),
                (right_hbm, right),
            )
        )
    ]
    for load in loads:
        load.start()

    barrier = pltpu.get_barrier_semaphore()
    c_next, c_last = lax.rem(c + 1, canals), lax.rem(c + canals - 1, canals)
    k_next, k_last = lax.rem(k + 1, crosses), lax.rem(k + crosses - 1, crosses)

    def greet(device):
        pl.semaphore_signal(barrier, inc=1, device_id=device, device_id_type=MESH)

    def row_mate(i):
        return 4 * (c // 4) + lax.rem(c + i, 4)

    greet((c_next, k))
    greet((c_last, k))
    for i in range(1, canals // 4):
        greet((lax.rem(c + 4 * i, canals), k))
    for i in range(1, crosses):
        greet((c, lax.rem(k + i, crosses)))
    for i in range(1, 4):
        greet((row_mate(i), k))
    for load in loads:
        load.wait()

    for x in range(2):
        flag = iblank[x]
        live = (flag != 0).astype(F32)
        weight[x] = jnp.where(flag == 1, step_scale[x], 0.0)
        for v in range(NVAR):
            cells = conserved[x, v] * live
            known[x, v, 8:24, :] = cells
            low_out[x, v] = cells[0:2]
            high_out[x, v] = cells[14:16]

    pl.semaphore_wait(barrier, 2 + canals // 4 - 1 + crosses - 1 + 3)

    def lanes(ref, b):
        return ref.at[:, :, :, pl.ds(b * block, block)]

    transfers = [(high_out, low_in, (c, k_next)), (low_out, high_in, (c, k_last))]
    for b in range(blocks):
        own = known.at[:, :, pl.ds(8, 16), pl.ds(b * block, block)]
        transfers.append((own, lanes(before, b), (c_next, k)))
        transfers.append((own, lanes(after, b), (c_last, k)))
    halo = []
    for number, (source, target, device) in enumerate(transfers):
        copy = pltpu.make_async_remote_copy(
            src_ref=source,
            dst_ref=target,
            send_sem=halo_send.at[number],
            recv_sem=halo_recv.at[number],
            device_id=device,
            device_id_type=MESH,
        )
        copy.start()
        halo.append(copy)

    for i in range(1, 4):
        pl.semaphore_signal(entered, inc=1, device_id=(row_mate(i), k), device_id_type=MESH)

    lane = lax.broadcasted_iota(jnp.int32, TILE, 1)
    sub = lax.broadcasted_iota(jnp.int32, TILE, 0)
    upper_half = sub < 4
    zero = jnp.zeros(TILE, F32)

    def pack(matrices, target, b):
        first, second = matrices[0].T, matrices[1].T
        for n in range(block // 8):
            one, two = first[8 * n : 8 * n + 8], second[8 * n : 8 * n + 8]
            chunk = b * per + 2 * n
            target[chunk] = jnp.where(upper_half, one, pltpu.roll(two, 4, 0))
            target[chunk + 1] = jnp.where(upper_half, pltpu.roll(one, 4, 0), two)

    halo[0].wait_recv()
    halo[1].wait_recv()
    has_last, has_next = c > 0, c < canals - 1
    low_mask, high_mask = k > 0, k < crosses - 1
    zi = lax.broadcasted_iota(jnp.int32, (16, depth), 1)
    for x in range(2):
        for v in range(NVAR):
            known[x, v, 6:8, :] = jnp.where(low_mask, low_in[x, v], 0.0)
            known[x, v, 24:26, :] = jnp.where(high_mask, high_in[x, v], 0.0)
            here = known[x, v, 8:24, :]
            z_half = 0.5 * speeds[2, v]
            up_one = jnp.where(zi < depth - 1, pltpu.roll(here, depth - 1, 1), 0.0)
            up_two = jnp.where(zi < depth - 2, pltpu.roll(here, depth - 2, 1), 0.0)
            down_one = jnp.where(zi >= 1, pltpu.roll(here, 1, 1), 0.0)
            down_two = jnp.where(zi >= 2, pltpu.roll(here, 2, 1), 0.0)
            flux = (z_half - 0.125) * up_one - (z_half + 0.125) * down_one
            outer = up_two + down_two
            cross_half = 0.5 * speeds[1, v]
            flux += (cross_half - 0.125) * known[x, v, 9:25, :]
            flux -= (cross_half + 0.125) * known[x, v, 7:23, :]
            outer += known[x, v, 10:26, :] + known[x, v, 6:22, :]
            partial[x, v] = flux + (outer + 18.0 * here) * (1.0 / 32.0)

    def send_tile(source, target, device, number):
        pltpu.make_async_remote_copy(
            src_ref=source,
            dst_ref=target,
            send_sem=send_sems.at[number],
            recv_sem=recv_sems.at[number],
            device_id=device,
            device_id_type=MESH,
        ).start()

    def wait_for(ref, count, sem):
        part = ref.at[pl.ds(0, count)]
        pltpu.make_async_copy(part, part, sem).wait()

    def retreat(p_rows, q_rows, g_rows, total, span, x_one, x_two, finish):
        def block(base, length, x_one, x_two):
            for i in range(length - 1, -1, -1):
                n = base + i
                solved = (g_rows[n] - q_rows[n] * x_two) - p_rows[n] * x_one
                g_rows[n] = solved
                x_one, x_two = solved, x_one
            return x_one, x_two

        start = total - span
        state = block(start, span - 1, x_one, x_two)
        finish(start)

        def more(i, state):
            base = total - span * (i + 2)
            state = block(base, span, *state)
            finish(base)
            return state

        lax.fori_loop(0, total // span - 1, more, state)

    pl.semaphore_wait(entered, 3)
    middle = c // blocks

    def to_canal(b, m):
        other = blocks * m + b
        send_tile(send_one.at[b * per + m], recv_one.at[c], (other, k), 0)

    for b in range(blocks):
        halo[2 + 2 * b].wait_recv()
        halo[3 + 2 * b].wait_recv()
        here = slice(b * block, (b + 1) * block)
        for x in range(2):
            fluxes = []
            for v in range(NVAR):
                if x == 0:
                    minus_one = jnp.where(has_last, before[1, v, :, here], 0.0)
                    minus_two = jnp.where(has_last, before[0, v, :, here], 0.0)
                    plus_one = known[1, v, 8:24, here]
                    plus_two = jnp.where(has_next, after[0, v, :, here], 0.0)
                else:
                    minus_one = known[0, v, 8:24, here]
                    minus_two = jnp.where(has_last, before[1, v, :, here], 0.0)
                    plus_one = jnp.where(has_next, after[0, v, :, here], 0.0)
                    plus_two = jnp.where(has_next, after[1, v, :, here], 0.0)
                canal_half = 0.5 * speeds[0, v]
                flux = (canal_half - 0.125) * plus_one - (canal_half + 0.125) * minus_one
                fluxes.append(partial[x, v, :, here] + (flux + (plus_two + minus_two) * (1.0 / 32.0)))
            scale = weight[x, :, here]
            for v in range(NVAR):
                mixed = left[v, 0] * fluxes[0]
                for u in range(1, NVAR):
                    mixed += left[v, u] * fluxes[u]
                rows[x, 16 * v : 16 * v + 16, here] = -(scale * mixed)
            rows[x, 112:128, here] = scale
        pack([rows[x, :, here] for x in range(2)], send_one, b)

        def send_canal(i, carry):
            for sign in (1, -1):
                to_canal(b, lax.rem(middle + sign * (per // 2 - i) + per, per))
            return carry

        to_canal(b, lax.rem(middle + per // 2, per))
        lax.fori_loop(1, per // 2, send_canal, 0, unroll=True)
        mine_now = lax.rem(c, blocks) == b

        @pl.when(mine_now)
        def keep_own():
            pltpu.make_async_copy(
                send_one.at[b * per + middle], recv_one.at[c], recv_sems.at[0]
            ).start()

        @pl.when(jnp.logical_not(mine_now))
        def send_near():
            to_canal(b, middle)

    for b in range(blocks):
        here = slice(b * block, (b + 1) * block)
        pack([jnp.concatenate([weight[x, :, here]] * 8, axis=0) for x in range(2)], vertical_weight, b)
    v_top = lax.rem(sub, 4) == 0
    v_lower, v_centre, v_upper = coefficients(speeds, 2, lane // 16, v_top)

    def v_pick(ref, n, step):
        near, far = ref[n], ref[canals - 1 - n]
        if step:
            near = pltpu.roll(near, 8 - step, 0)
        if step != 2:
            far = pltpu.roll(far, (step + 6) % 8, 0)
        return jnp.where(v_top, near, far)

    def v_factor(m, carry):
        p_one, q_one, p_two, q_two = carry
        for part in range(8):
            n, step = 2 * m + part // 4, part % 4
            w = v_pick(vertical_weight, n, step)
            inverse, multiplier, p_new, q_new = factor(
                w, v_lower, v_centre, v_upper, p_one, q_one, p_two, q_two
            )
            v_inverse[4 * n + step] = inverse
            v_multiplier[4 * n + step] = multiplier
            v_p[4 * n + step] = p_new
            v_q[4 * n + step] = q_new
            p_one, q_one, p_two, q_two = p_new, q_new, p_one, q_one
        return p_one, q_one, p_two, q_two

    lax.fori_loop(0, half // 2, v_factor, (zero, zero, zero, zero))

    wait_for(recv_one, canals, recv_sems.at[0])

    c_lower, c_centre, c_upper = coefficients(speeds, 0, lane // 16, upper_half)
    is_weight = lane >= 112

    def widen(tile):
        w = jnp.where(is_weight, tile, 0.0)
        w += pltpu.roll(w, 16, 1)
        w += pltpu.roll(w, 32, 1)
        return w + pltpu.roll(w, 64, 1)

    def c_forward(i, carry):
        g_one, p_one, q_one, g_two, p_two, q_two = carry
        for m in range(8):
            n = 8 * i + m
            near, far = recv_one[n], recv_one[canals - 1 - n]
            outer = jnp.where(upper_half, near, far)
            inner = pltpu.roll(jnp.where(upper_half, far, near), 4, 0)
            for step, source in enumerate((outer, inner)):
                w = widen(source)
                inverse, multiplier, p_new, q_new = factor(
                    w, c_lower, c_centre, c_upper, p_one, q_one, p_two, q_two
                )
                g_new = (source * inverse - q_new * g_two) - multiplier * g_one
                work_g[2 * n + step] = g_new
                work_p[2 * n + step] = p_new
                work_q[2 * n + step] = q_new
                g_one, p_one, q_one, g_two, p_two, q_two = g_new, p_new, q_new, g_one, p_one, q_one
        return g_one, p_one, q_one, g_two, p_two, q_two

    g_one, p_one, q_one, g_two, p_two, q_two = lax.fori_loop(0, half // 8, c_forward, (zero,) * 6)

    def c_swap(a):
        return pltpu.roll(a, 4, 0)

    x_one = join(c_swap, g_one, g_two, p_one, q_one, p_two, q_two)
    work_g[canals - 1] = x_one

    def c_restore(start):
        for m in range(8):
            n = start // 2 + m
            outer, inner = work_g[start + 2 * m], pltpu.roll(work_g[start + 2 * m + 1], 4, 0)
            for pair, tile in (
                (n, jnp.where(upper_half, outer, inner)),
                (canals - 1 - n, jnp.where(upper_half, inner, outer)),
            ):
                group, place = partner_of(pair, c, crosses)
                send_two[group * places + place] = jnp.where(is_weight, recv_one[pair], tile)

    retreat(work_p, work_q, work_g, canals, 16, x_one, c_swap(x_one), c_restore)

    def group_of(ref, position):
        return ref.at[pl.ds(position * places, places)]

    def send_cross(i, carry):
        other = lax.rem(k + i, crosses)
        send_tile(group_of(send_two, other), group_of(recv_two, k), (c, other), 1)
        return carry

    lax.fori_loop(1, crosses, send_cross, 0)
    pltpu.make_async_copy(group_of(send_two, k), group_of(recv_two, k), recv_sems.at[1]).start()
    wait_for(recv_two, canals, recv_sems.at[1])

    count = crosses // 2
    lines = 8 * places
    for pair in range(count):
        near = recv_two[pair * places : (pair + 1) * places].reshape(lines, 128)
        other = crosses - 1 - pair
        far = recv_two[other * places : (other + 1) * places].reshape(lines, 128)
        turned[pair] = jnp.concatenate([near, far], axis=0).T

    x_top = lane < lines
    x_lower, x_centre, x_upper = coefficients(speeds, 1, sub, x_top)

    def x_forward(pair, carry):
        g_one, p_one, q_one, g_two, p_two, q_two = carry
        for y in range(16):
            source = jnp.where(
                x_top,
                turned[pair, pl.ds(y, 8, stride=16), :],
                turned[pair, pl.ds(15 - y, 8, stride=16), :],
            )
            w = jnp.broadcast_to(source[7:8], TILE)
            inverse, multiplier, p_new, q_new = factor(
                w, x_lower, x_centre, x_upper, p_one, q_one, p_two, q_two
            )
            g_new = (source * inverse - q_new * g_two) - multiplier * g_one
            work_g[16 * pair + y] = g_new
            work_p[16 * pair + y] = p_new
            work_q[16 * pair + y] = q_new
            g_one, p_one, q_one, g_two, p_two, q_two = g_new, p_new, q_new, g_one, p_one, q_one
        return g_one, p_one, q_one, g_two, p_two, q_two

    g_one, p_one, q_one, g_two, p_two, q_two = lax.fori_loop(0, count, x_forward, (zero,) * 6)

    def x_swap(a):
        return pltpu.roll(a, lines, 1)

    x_one = join(x_swap, g_one, g_two, p_one, q_one, p_two, q_two)
    work_g[16 * count - 1] = x_one

    chunk_here = c // blocks + per * lax.rem(c, blocks)

    def send_home(pair):
        def one(i, carry):
            place = lax.rem(i + c, places)
            target = pair_of(k, c, place, crosses)
            for other in (pair, crosses - 1 - pair):
                source = send_three.at[other * places + place]
                itself = jnp.logical_and(target == c, other == k)

                @pl.when(itself)
                def keep():
                    pltpu.make_async_copy(source, recv_three.at[chunk_here], recv_sems.at[2]).start()

                @pl.when(jnp.logical_not(itself))
                def send():
                    send_tile(source, recv_three.at[chunk_here], (target, other), 2)

            return carry

        lax.fori_loop(0, places, one, 0, unroll=True)

    def x_restore(start):
        pair = start // 16
        for y in range(16):
            turned[pair, pl.ds(y, 8, stride=16), :] = jnp.where(
                x_top, work_g[start + y], work_g[start + 15 - y]
            )
        back = turned[pair].T
        for block in range(places):
            at = 8 * block
            send_three[pair * places + block] = back[at : at + 8]
            send_three[(crosses - 1 - pair) * places + block] = back[lines + at : lines + at + 8]
        send_home(pair)

    retreat(work_p, work_q, work_g, 16 * count, 16, x_one, x_swap(x_one), x_restore)
    wait_for(recv_three, canals, recv_sems.at[2])

    def v_forward(m, carry):
        g_one, g_two = carry
        for step in range(16):
            i = 16 * m + step
            source = v_pick(recv_three, 4 * m + step // 4, step % 4)
            g_new = (source * v_inverse[i] - v_q[i] * g_two) - v_multiplier[i] * g_one
            v_g[i] = g_new
            g_one, g_two = g_new, g_one
        return g_one, g_two

    g_one, g_two = lax.fori_loop(0, half // 4, v_forward, (zero, zero))

    def v_swap(a):
        return jnp.where(v_top, pltpu.roll(a, 7, 0), pltpu.roll(a, 1, 0))

    last = 2 * canals - 1
    x_one = join(v_swap, g_one, g_two, v_p[last], v_q[last], v_p[last - 1], v_q[last - 1])
    v_g[last] = x_one

    place_of = lax.rem(sub, 4)

    def v_chunk(n):
        near, far = [], []
        for part in range(2):
            base = 8 * n + 4 * part
            near_tile = v_g[base]
            far_tile = pltpu.roll(v_g[base], 2, 0)
            for step in range(1, 4):
                near_tile = jnp.where(
                    place_of == step, pltpu.roll(v_g[base + step], step, 0), near_tile
                )
                far_tile = jnp.where(
                    place_of == 3 - step,
                    pltpu.roll(v_g[base + step], (10 - step) % 8, 0),
                    far_tile,
                )
            near.append(near_tile)
            far.append(far_tile)
        far = far[::-1]
        at = pl.multiple_of(8 * n, 8)
        end = pl.multiple_of(depth - 8 - 8 * n, 8)
        for start, (one, two) in ((at, near), (end, far)):
            upright[0, pl.ds(start, 8), :] = jnp.where(upper_half, one, pltpu.roll(two, 4, 0))
            upright[1, pl.ds(start, 8), :] = jnp.where(upper_half, pltpu.roll(one, 4, 0), two)

    def v_restore(start):
        v_chunk(start // 8)
        v_chunk(start // 8 + 1)

    retreat(v_p, v_q, v_g, 2 * canals, 16, x_one, v_swap(x_one), v_restore)

    outgoing = []
    for x in range(2):
        for b in range(blocks):
            third = upright[x, b * block : (b + 1) * block, :].T
            for v in range(NVAR):
                mixed = right[v, 0] * third[0:16]
                for u in range(1, NVAR):
                    mixed += right[v, u] * third[16 * u : 16 * u + 16]
                result[x, v, :, b * block : (b + 1) * block] = mixed
            finished = pltpu.make_async_copy(
                result.at[x, :, :, pl.ds(b * block, block)],
                update.at[x, :, :, pl.ds(b * block, block)],
                out_sems.at[x * blocks + b],
            )
            finished.start()
            outgoing.append(finished)

    for copy in halo:
        copy.wait_send()
    wait_for(send_one, canals - 1, send_sems.at[0])
    wait_for(send_two, canals - places, send_sems.at[1])
    mine, unused = partner_of(c, c, crosses)

    @pl.when(mine == k)
    def sent_fewer():
        wait_for(send_three, canals - 1, send_sems.at[2])

    @pl.when(mine != k)
    def sent_all():
        wait_for(send_three, canals, send_sems.at[2])

    for finished in outgoing:
        finished.wait()


def solution(mesh):
    canals, crosses = mesh.shape["canal"], mesh.shape["cross"]
    depth = 4 * canals
    cells = (2, NVAR, 16, depth)
    tiles = (canals,) + TILE
    transfers = 2 + 2 * (depth // min(depth, 128))

    def shards(conserved, iblank, step_scale, speeds, left_vectors, right_vectors):
        anywhere = pl.BlockSpec(memory_space=pl.ANY)

        def held(*shape):
            return pltpu.VMEM(shape, F32)

        return pl.pallas_call(
            functools.partial(kernel, canals, crosses),
            out_shape=jax.ShapeDtypeStruct(cells, F32),
            in_specs=[anywhere] * 6,
            out_specs=anywhere,
            scratch_shapes=[
                held(*cells),
                pltpu.VMEM((2, 16, depth), jnp.int32),
                held(2, 16, depth),
                pltpu.SMEM((3, NVAR), F32),
                pltpu.SMEM((NVAR, NVAR), F32),
                pltpu.SMEM((NVAR, NVAR), F32),
                held(2, NVAR, 32, depth),
                held(2, 16, depth),
                held(2, NVAR, 2, depth),
                held(2, NVAR, 2, depth),
                held(2, NVAR, 2, depth),
                held(2, NVAR, 2, depth),
                held(*cells),
                held(*cells),
                held(*cells),
                held(2, 128, depth),
                held(*tiles),
                held(*tiles),
                held(*tiles),
                held(*tiles),
                held(crosses // 2, 128, 16 * (canals // crosses)),
                held(*tiles),
                held(*tiles),
                held(*tiles),
                held(2, depth, 128),
                held(*cells),
                held(2 * canals, *TILE),
                held(2 * canals, *TILE),
                held(2 * canals, *TILE),
                held(2 * canals, *TILE),
                held(max(canals, 8 * crosses), *TILE),
                held(max(canals, 8 * crosses), *TILE),
                held(max(canals, 8 * crosses), *TILE),
                held(2 * canals, *TILE),
                pltpu.SemaphoreType.DMA((6,)),
                pltpu.SemaphoreType.DMA((transfers,)),
                pltpu.SemaphoreType.DMA((transfers,)),
                pltpu.SemaphoreType.DMA((3,)),
                pltpu.SemaphoreType.DMA((3,)),
                pltpu.SemaphoreType.DMA((transfers - 2,)),
                pltpu.SemaphoreType.REGULAR,
            ],
            compiler_params=pltpu.CompilerParams(
                collective_id=0, has_side_effects=True, vmem_limit_bytes=60 * 1024 * 1024
            ),
        )(conserved, iblank, step_scale, speeds, left_vectors, right_vectors)

    return jax.shard_map(
        shards,
        mesh=mesh,
        in_specs=(
            P("canal", None, "cross", None),
            P("canal", "cross", None),
            P("canal", "cross", None),
            P(),
            P(),
            P(),
        ),
        out_specs=P("canal", None, "cross", None),
        check_vma=False,
    )
```

```python
import functools

import jax
import jax.numpy as jnp
from jax import lax
from jax.experimental import pallas as pl
from jax.experimental.pallas import tpu as pltpu
from jax.sharding import PartitionSpec as P

MESH = pl.DeviceIdType.MESH
F32 = jnp.float32
NVAR = 7
TILE = (8, 128)


def turn_of(canal, crosses):
    return lax.rem(canal // 4, crosses)


def partner_of(pair, canal, crosses):
    return lax.rem(lax.rem(pair, crosses) + turn_of(canal, crosses), crosses), pair // crosses


def pair_of(group, canal, place, crosses):
    return crosses * place + lax.rem(group - turn_of(canal, crosses) + crosses, crosses)


def factor(w, lower, centre, upper, p_one, q_one, p_two, q_two):
    damping = 0.25 * w
    reduced = w * (0.25 * p_two - lower)
    pivot = (1.0 + centre * w + damping * q_two) - reduced * p_one
    inverse = 1.0 / pivot
    q_new = -damping * inverse
    p_new = -(upper * w + reduced * q_one) * inverse
    return inverse, reduced * inverse, p_new, q_new


def join(swap, g_one, g_two, p_one, q_one, p_two, q_two):
    alpha = 1.0 - q_one * swap(q_two)
    beta = p_one - q_one * swap(p_two)
    gamma = g_one - q_one * swap(g_two)
    alpha_far, beta_far, gamma_far = swap(alpha), swap(beta), swap(gamma)
    return (gamma * alpha_far - beta * gamma_far) / (alpha * alpha_far - beta * beta_far)


def spread(speeds_ref, direction, index):
    forward = jnp.zeros(index.shape, F32)
    backward = jnp.zeros(index.shape, F32)
    for v in range(NVAR):
        speed = speeds_ref[direction, v]
        forward = jnp.where(index == v, jnp.maximum(speed, 0.0), forward)
        backward = jnp.where(index == v, jnp.maximum(-speed, 0.0), backward)
    return forward, backward


def coefficients(speeds_ref, direction, index, top):
    forward, backward = spread(speeds_ref, direction, index)
    lower = jnp.where(top, forward, backward) + 0.25
    upper = jnp.where(top, backward, forward) + 0.25
    return lower, 1.0 + forward + backward, upper


def kernel(
    canals,
    crosses,
    conserved_hbm,
    iblank_hbm,
    step_scale_hbm,
    speeds_hbm,
    left_hbm,
    right_hbm,
    update,
    conserved,
    iblank,
    step_scale,
    speeds,
    left,
    right,
    known,
    weight,
    low_out,
    high_out,
    low_in,
    high_in,
    before,
    after,
    partial,
    rows,
    send_one,
    recv_one,
    send_two,
    recv_two,
    turned,
    send_three,
    recv_three,
    vertical_weight,
    upright,
    result,
    v_inverse,
    v_multiplier,
    v_p,
    v_q,
    work_p,
    work_q,
    work_g,
    v_g,
    load_sems,
    halo_send,
    halo_recv,
    send_sems,
    recv_sems,
    out_sems,
    entered,
):
    depth = 4 * canals
    block = min(depth, 128)
    blocks = depth // block
    places = canals // crosses
    half = canals // 2
    per = canals // blocks
    c = lax.axis_index("canal")
    k = lax.axis_index("cross")

    loads = [
        pltpu.make_async_copy(source, target, load_sems.at[number])
        for number, (source, target) in enumerate(
            (
                (iblank_hbm, iblank),
                (conserved_hbm, conserved),
                (step_scale_hbm, step_scale),
                (speeds_hbm, speeds),
                (left_hbm, left),
                (right_hbm, right),
            )
        )
    ]
    for load in loads:
        load.start()

    barrier = pltpu.get_barrier_semaphore()
    c_next, c_last = lax.rem(c + 1, canals), lax.rem(c + canals - 1, canals)
    k_next, k_last = lax.rem(k + 1, crosses), lax.rem(k + crosses - 1, crosses)

    def greet(device):
        pl.semaphore_signal(barrier, inc=1, device_id=device, device_id_type=MESH)

    def row_mate(i):
        return 4 * (c // 4) + lax.rem(c + i, 4)

    for i in sorted(range(1, canals // 4), key=lambda i: abs(i - canals // 8)):
        greet((lax.rem(c + 4 * i, canals), k))
    greet((c_next, k))
    greet((c_last, k))
    for i in range(1, crosses):
        greet((c, lax.rem(k + i, crosses)))
    for i in range(1, 4):
        greet((row_mate(i), k))
    for load in loads:
        load.wait()

    for x in range(2):
        flag = iblank[x]
        live = (flag != 0).astype(F32)
        weight[x] = jnp.where(flag == 1, step_scale[x], 0.0)
        for v in range(NVAR):
            cells = conserved[x, v] * live
            known[x, v, 8:24, :] = cells
            low_out[x, v] = cells[0:2]
            high_out[x, v] = cells[14:16]

    pl.semaphore_wait(barrier, 2 + canals // 4 - 1 + crosses - 1 + 3)

    def lanes(ref, b):
        return ref.at[:, :, :, pl.ds(b * block, block)]

    transfers = [(high_out, low_in, (c, k_next)), (low_out, high_in, (c, k_last))]
    for b in range(blocks):
        own = known.at[:, :, pl.ds(8, 16), pl.ds(b * block, block)]
        transfers.append((own, lanes(before, b), (c_next, k)))
        transfers.append((own, lanes(after, b), (c_last, k)))
    halo = []
    for number, (source, target, device) in enumerate(transfers):
        copy = pltpu.make_async_remote_copy(
            src_ref=source,
            dst_ref=target,
            send_sem=halo_send.at[number],
            recv_sem=halo_recv.at[number],
            device_id=device,
            device_id_type=MESH,
        )
        copy.start()
        halo.append(copy)

    for i in range(1, 4):
        pl.semaphore_signal(entered, inc=1, device_id=(row_mate(i), k), device_id_type=MESH)

    lane = lax.broadcasted_iota(jnp.int32, TILE, 1)
    sub = lax.broadcasted_iota(jnp.int32, TILE, 0)
    upper_half = sub < 4
    zero = jnp.zeros(TILE, F32)

    def pack(matrices, target, b):
        first, second = matrices[0].T, matrices[1].T
        for n in range(block // 8):
            one, two = first[8 * n : 8 * n + 8], second[8 * n : 8 * n + 8]
            chunk = b * per + 2 * n
            target[chunk] = jnp.where(upper_half, one, pltpu.roll(two, 4, 0))
            target[chunk + 1] = jnp.where(upper_half, pltpu.roll(one, 4, 0), two)

    halo[0].wait_recv()
    halo[1].wait_recv()
    has_last, has_next = c > 0, c < canals - 1
    low_mask, high_mask = k > 0, k < crosses - 1
    zi = lax.broadcasted_iota(jnp.int32, (16, depth), 1)
    for x in range(2):
        for v in range(NVAR):
            known[x, v, 6:8, :] = jnp.where(low_mask, low_in[x, v], 0.0)
            known[x, v, 24:26, :] = jnp.where(high_mask, high_in[x, v], 0.0)
            here = known[x, v, 8:24, :]
            z_half = 0.5 * speeds[2, v]
            up_one = jnp.where(zi < depth - 1, pltpu.roll(here, depth - 1, 1), 0.0)
            up_two = jnp.where(zi < depth - 2, pltpu.roll(here, depth - 2, 1), 0.0)
            down_one = jnp.where(zi >= 1, pltpu.roll(here, 1, 1), 0.0)
            down_two = jnp.where(zi >= 2, pltpu.roll(here, 2, 1), 0.0)
            flux = (z_half - 0.125) * up_one - (z_half + 0.125) * down_one
            outer = up_two + down_two
            cross_half = 0.5 * speeds[1, v]
            flux += (cross_half - 0.125) * known[x, v, 9:25, :]
            flux -= (cross_half + 0.125) * known[x, v, 7:23, :]
            outer += known[x, v, 10:26, :] + known[x, v, 6:22, :]
            partial[x, v] = flux + (outer + 18.0 * here) * (1.0 / 32.0)

    def send_tile(source, target, device, number):
        pltpu.make_async_remote_copy(
            src_ref=source,
            dst_ref=target,
            send_sem=send_sems.at[number],
            recv_sem=recv_sems.at[number],
            device_id=device,
            device_id_type=MESH,
        ).start()

    def wait_for(ref, count, sem):
        part = ref.at[pl.ds(0, count)]
        pltpu.make_async_copy(part, part, sem).wait()

    def retreat(p_rows, q_rows, g_rows, total, span, x_one, x_two, finish):
        def block(base, length, x_one, x_two):
            for i in range(length - 1, -1, -1):
                n = base + i
                solved = (g_rows[n] - q_rows[n] * x_two) - p_rows[n] * x_one
                g_rows[n] = solved
                x_one, x_two = solved, x_one
            return x_one, x_two

        start = total - span
        state = block(start, span - 1, x_one, x_two)
        finish(start)

        def more(i, state):
            base = total - span * (i + 2)
            state = block(base, span, *state)
            finish(base)
            return state

        lax.fori_loop(0, total // span - 1, more, state)

    pl.semaphore_wait(entered, 3)
    middle = c // blocks

    def to_canal(b, m):
        other = blocks * m + b
        send_tile(send_one.at[b * per + m], recv_one.at[c], (other, k), 0)

    for b in range(blocks):
        halo[2 + 2 * b].wait_recv()
        halo[3 + 2 * b].wait_recv()
        here = slice(b * block, (b + 1) * block)
        for x in range(2):
            fluxes = []
            for v in range(NVAR):
                if x == 0:
                    minus_one = jnp.where(has_last, before[1, v, :, here], 0.0)
                    minus_two = jnp.where(has_last, before[0, v, :, here], 0.0)
                    plus_one = known[1, v, 8:24, here]
                    plus_two = jnp.where(has_next, after[0, v, :, here], 0.0)
                else:
                    minus_one = known[0, v, 8:24, here]
                    minus_two = jnp.where(has_last, before[1, v, :, here], 0.0)
                    plus_one = jnp.where(has_next, after[0, v, :, here], 0.0)
                    plus_two = jnp.where(has_next, after[1, v, :, here], 0.0)
                canal_half = 0.5 * speeds[0, v]
                flux = (canal_half - 0.125) * plus_one - (canal_half + 0.125) * minus_one
                fluxes.append(partial[x, v, :, here] + (flux + (plus_two + minus_two) * (1.0 / 32.0)))
            scale = weight[x, :, here]
            for v in range(NVAR):
                mixed = left[v, 0] * fluxes[0]
                for u in range(1, NVAR):
                    mixed += left[v, u] * fluxes[u]
                rows[x, 16 * v : 16 * v + 16, here] = -(scale * mixed)
            rows[x, 112:128, here] = scale
        pack([rows[x, :, here] for x in range(2)], send_one, b)

        def send_canal(i, carry):
            for sign in (1, -1):
                to_canal(b, lax.rem(middle + sign * (per // 2 - i) + per, per))
            return carry

        to_canal(b, lax.rem(middle + per // 2, per))
        lax.fori_loop(1, per // 2, send_canal, 0)
        mine_now = lax.rem(c, blocks) == b

        @pl.when(mine_now)
        def keep_own():
            pltpu.make_async_copy(
                send_one.at[b * per + middle], recv_one.at[c], recv_sems.at[0]
            ).start()

        @pl.when(jnp.logical_not(mine_now))
        def send_near():
            to_canal(b, middle)

    for b in range(blocks):
        here = slice(b * block, (b + 1) * block)
        pack([jnp.concatenate([weight[x, :, here]] * 8, axis=0) for x in range(2)], vertical_weight, b)
    v_top = lax.rem(sub, 4) == 0
    v_lower, v_centre, v_upper = coefficients(speeds, 2, lane // 16, v_top)

    def v_pick(ref, n, step):
        near, far = ref[n], ref[canals - 1 - n]
        if step:
            near = pltpu.roll(near, 8 - step, 0)
        if step != 2:
            far = pltpu.roll(far, (step + 6) % 8, 0)
        return jnp.where(v_top, near, far)

    def v_factor(m, carry):
        p_one, q_one, p_two, q_two = carry
        for part in range(8):
            n, step = 2 * m + part // 4, part % 4
            w = v_pick(vertical_weight, n, step)
            inverse, multiplier, p_new, q_new = factor(
                w, v_lower, v_centre, v_upper, p_one, q_one, p_two, q_two
            )
            v_inverse[4 * n + step] = inverse
            v_multiplier[4 * n + step] = multiplier
            v_p[4 * n + step] = p_new
            v_q[4 * n + step] = q_new
            p_one, q_one, p_two, q_two = p_new, q_new, p_one, q_one
        return p_one, q_one, p_two, q_two

    lax.fori_loop(0, half // 2, v_factor, (zero, zero, zero, zero))

    wait_for(recv_one, canals, recv_sems.at[0])

    c_lower, c_centre, c_upper = coefficients(speeds, 0, lane // 16, upper_half)
    is_weight = lane >= 112

    def widen(tile):
        w = jnp.where(is_weight, tile, 0.0)
        w += pltpu.roll(w, 16, 1)
        w += pltpu.roll(w, 32, 1)
        return w + pltpu.roll(w, 64, 1)

    def c_forward(i, carry):
        g_one, p_one, q_one, g_two, p_two, q_two = carry
        for m in range(8):
            n = 8 * i + m
            near, far = recv_one[n], recv_one[canals - 1 - n]
            outer = jnp.where(upper_half, near, far)
            inner = pltpu.roll(jnp.where(upper_half, far, near), 4, 0)
            for step, source in enumerate((outer, inner)):
                w = widen(source)
                inverse, multiplier, p_new, q_new = factor(
                    w, c_lower, c_centre, c_upper, p_one, q_one, p_two, q_two
                )
                g_new = (source * inverse - q_new * g_two) - multiplier * g_one
                work_g[2 * n + step] = g_new
                work_p[2 * n + step] = p_new
                work_q[2 * n + step] = q_new
                g_one, p_one, q_one, g_two, p_two, q_two = g_new, p_new, q_new, g_one, p_one, q_one
        return g_one, p_one, q_one, g_two, p_two, q_two

    g_one, p_one, q_one, g_two, p_two, q_two = lax.fori_loop(0, half // 8, c_forward, (zero,) * 6)

    def c_swap(a):
        return pltpu.roll(a, 4, 0)

    x_one = join(c_swap, g_one, g_two, p_one, q_one, p_two, q_two)
    work_g[canals - 1] = x_one

    def c_restore(start):
        for m in range(8):
            n = start // 2 + m
            outer, inner = work_g[start + 2 * m], pltpu.roll(work_g[start + 2 * m + 1], 4, 0)
            for pair, tile in (
                (n, jnp.where(upper_half, outer, inner)),
                (canals - 1 - n, jnp.where(upper_half, inner, outer)),
            ):
                group, place = partner_of(pair, c, crosses)
                send_two[group * places + place] = jnp.where(is_weight, recv_one[pair], tile)

    retreat(work_p, work_q, work_g, canals, 16, x_one, c_swap(x_one), c_restore)

    def group_of(ref, position):
        return ref.at[pl.ds(position * places, places)]

    def send_cross(i, carry):
        other = lax.rem(k + i, crosses)
        send_tile(group_of(send_two, other), group_of(recv_two, k), (c, other), 1)
        return carry

    lax.fori_loop(1, crosses, send_cross, 0)
    pltpu.make_async_copy(group_of(send_two, k), group_of(recv_two, k), recv_sems.at[1]).start()
    wait_for(recv_two, canals, recv_sems.at[1])

    count = crosses // 2
    lines = 8 * places
    for pair in range(count):
        near = recv_two[pair * places : (pair + 1) * places].reshape(lines, 128)
        other = crosses - 1 - pair
        far = recv_two[other * places : (other + 1) * places].reshape(lines, 128)
        turned[pair] = jnp.concatenate([near, far], axis=0).T

    x_top = lane < lines
    x_lower, x_centre, x_upper = coefficients(speeds, 1, sub, x_top)

    def x_forward(pair, carry):
        g_one, p_one, q_one, g_two, p_two, q_two = carry
        for y in range(16):
            source = jnp.where(
                x_top,
                turned[pair, pl.ds(y, 8, stride=16), :],
                turned[pair, pl.ds(15 - y, 8, stride=16), :],
            )
            w = jnp.broadcast_to(source[7:8], TILE)
            inverse, multiplier, p_new, q_new = factor(
                w, x_lower, x_centre, x_upper, p_one, q_one, p_two, q_two
            )
            g_new = (source * inverse - q_new * g_two) - multiplier * g_one
            work_g[16 * pair + y] = g_new
            work_p[16 * pair + y] = p_new
            work_q[16 * pair + y] = q_new
            g_one, p_one, q_one, g_two, p_two, q_two = g_new, p_new, q_new, g_one, p_one, q_one
        return g_one, p_one, q_one, g_two, p_two, q_two

    g_one, p_one, q_one, g_two, p_two, q_two = lax.fori_loop(0, count, x_forward, (zero,) * 6)

    def x_swap(a):
        return pltpu.roll(a, lines, 1)

    x_one = join(x_swap, g_one, g_two, p_one, q_one, p_two, q_two)
    work_g[16 * count - 1] = x_one

    chunk_here = c // blocks + per * lax.rem(c, blocks)

    def send_home(pair):
        def one(i, carry):
            place = lax.rem(i + c, places)
            target = pair_of(k, c, place, crosses)
            for other in (pair, crosses - 1 - pair):
                source = send_three.at[other * places + place]
                itself = jnp.logical_and(target == c, other == k)

                @pl.when(itself)
                def keep():
                    pltpu.make_async_copy(source, recv_three.at[chunk_here], recv_sems.at[2]).start()

                @pl.when(jnp.logical_not(itself))
                def send():
                    send_tile(source, recv_three.at[chunk_here], (target, other), 2)

            return carry

        lax.fori_loop(0, places, one, 0)

    def x_restore(start):
        pair = start // 16
        for y in range(16):
            turned[pair, pl.ds(y, 8, stride=16), :] = jnp.where(
                x_top, work_g[start + y], work_g[start + 15 - y]
            )
        back = turned[pair].T
        for block in range(places):
            at = 8 * block
            send_three[pair * places + block] = back[at : at + 8]
            send_three[(crosses - 1 - pair) * places + block] = back[lines + at : lines + at + 8]
        send_home(pair)

    retreat(work_p, work_q, work_g, 16 * count, 16, x_one, x_swap(x_one), x_restore)
    wait_for(recv_three, canals, recv_sems.at[2])

    def v_forward(m, carry):
        g_one, g_two = carry
        for step in range(16):
            i = 16 * m + step
            source = v_pick(recv_three, 4 * m + step // 4, step % 4)
            g_new = (source * v_inverse[i] - v_q[i] * g_two) - v_multiplier[i] * g_one
            v_g[i] = g_new
            g_one, g_two = g_new, g_one
        return g_one, g_two

    g_one, g_two = lax.fori_loop(0, half // 4, v_forward, (zero, zero))

    def v_swap(a):
        return jnp.where(v_top, pltpu.roll(a, 7, 0), pltpu.roll(a, 1, 0))

    last = 2 * canals - 1
    x_one = join(v_swap, g_one, g_two, v_p[last], v_q[last], v_p[last - 1], v_q[last - 1])
    v_g[last] = x_one

    place_of = lax.rem(sub, 4)

    def v_chunk(n):
        near, far = [], []
        for part in range(2):
            base = 8 * n + 4 * part
            near_tile = v_g[base]
            far_tile = pltpu.roll(v_g[base], 2, 0)
            for step in range(1, 4):
                near_tile = jnp.where(
                    place_of == step, pltpu.roll(v_g[base + step], step, 0), near_tile
                )
                far_tile = jnp.where(
                    place_of == 3 - step,
                    pltpu.roll(v_g[base + step], (10 - step) % 8, 0),
                    far_tile,
                )
            near.append(near_tile)
            far.append(far_tile)
        far = far[::-1]
        at = pl.multiple_of(8 * n, 8)
        end = pl.multiple_of(depth - 8 - 8 * n, 8)
        for start, (one, two) in ((at, near), (end, far)):
            upright[0, pl.ds(start, 8), :] = jnp.where(upper_half, one, pltpu.roll(two, 4, 0))
            upright[1, pl.ds(start, 8), :] = jnp.where(upper_half, pltpu.roll(one, 4, 0), two)

    def v_restore(start):
        v_chunk(start // 8)
        v_chunk(start // 8 + 1)

    retreat(v_p, v_q, v_g, 2 * canals, 16, x_one, v_swap(x_one), v_restore)

    outgoing = []
    for x in range(2):
        for b in range(blocks):
            third = upright[x, b * block : (b + 1) * block, :].T
            for v in range(NVAR):
                mixed = right[v, 0] * third[0:16]
                for u in range(1, NVAR):
                    mixed += right[v, u] * third[16 * u : 16 * u + 16]
                result[x, v, :, b * block : (b + 1) * block] = mixed
            finished = pltpu.make_async_copy(
                result.at[x, :, :, pl.ds(b * block, block)],
                update.at[x, :, :, pl.ds(b * block, block)],
                out_sems.at[x * blocks + b],
            )
            finished.start()
            outgoing.append(finished)

    for copy in halo:
        copy.wait_send()
    wait_for(send_one, canals - 1, send_sems.at[0])
    wait_for(send_two, canals - places, send_sems.at[1])
    mine, unused = partner_of(c, c, crosses)

    @pl.when(mine == k)
    def sent_fewer():
        wait_for(send_three, canals - 1, send_sems.at[2])

    @pl.when(mine != k)
    def sent_all():
        wait_for(send_three, canals, send_sems.at[2])

    for finished in outgoing:
        finished.wait()


def solution(mesh):
    canals, crosses = mesh.shape["canal"], mesh.shape["cross"]
    depth = 4 * canals
    cells = (2, NVAR, 16, depth)
    tiles = (canals,) + TILE
    transfers = 2 + 2 * (depth // min(depth, 128))

    def shards(conserved, iblank, step_scale, speeds, left_vectors, right_vectors):
        anywhere = pl.BlockSpec(memory_space=pl.ANY)

        def held(*shape):
            return pltpu.VMEM(shape, F32)

        return pl.pallas_call(
            functools.partial(kernel, canals, crosses),
            out_shape=jax.ShapeDtypeStruct(cells, F32),
            in_specs=[anywhere] * 6,
            out_specs=anywhere,
            scratch_shapes=[
                held(*cells),
                pltpu.VMEM((2, 16, depth), jnp.int32),
                held(2, 16, depth),
                pltpu.SMEM((3, NVAR), F32),
                pltpu.SMEM((NVAR, NVAR), F32),
                pltpu.SMEM((NVAR, NVAR), F32),
                held(2, NVAR, 32, depth),
                held(2, 16, depth),
                held(2, NVAR, 2, depth),
                held(2, NVAR, 2, depth),
                held(2, NVAR, 2, depth),
                held(2, NVAR, 2, depth),
                held(*cells),
                held(*cells),
                held(*cells),
                held(2, 128, depth),
                held(*tiles),
                held(*tiles),
                held(*tiles),
                held(*tiles),
                held(crosses // 2, 128, 16 * (canals // crosses)),
                held(*tiles),
                held(*tiles),
                held(*tiles),
                held(2, depth, 128),
                held(*cells),
                held(2 * canals, *TILE),
                held(2 * canals, *TILE),
                held(2 * canals, *TILE),
                held(2 * canals, *TILE),
                held(max(canals, 8 * crosses), *TILE),
                held(max(canals, 8 * crosses), *TILE),
                held(max(canals, 8 * crosses), *TILE),
                held(2 * canals, *TILE),
                pltpu.SemaphoreType.DMA((6,)),
                pltpu.SemaphoreType.DMA((transfers,)),
                pltpu.SemaphoreType.DMA((transfers,)),
                pltpu.SemaphoreType.DMA((3,)),
                pltpu.SemaphoreType.DMA((3,)),
                pltpu.SemaphoreType.DMA((transfers - 2,)),
                pltpu.SemaphoreType.REGULAR,
            ],
            compiler_params=pltpu.CompilerParams(
                collective_id=0, has_side_effects=True, vmem_limit_bytes=60 * 1024 * 1024
            ),
        )(conserved, iblank, step_scale, speeds, left_vectors, right_vectors)

    return jax.shard_map(
        shards,
        mesh=mesh,
        in_specs=(
            P("canal", None, "cross", None),
            P("canal", "cross", None),
            P("canal", "cross", None),
            P(),
            P(),
            P(),
        ),
        out_specs=P("canal", None, "cross", None),
        check_vma=False,
    )
```
